512 devices in a mesh: ctx: 16 (over z, core), head: 32 (over x, y).
Axes of the slice: x: 4, y: 8, z: 8, core: 2. Of those that a mesh axis runs over, the one named last changes fastest.
Arguments:
- queries: bfloat16 [8192, 4096], P('ctx', 'head'), may hold values from -180 to 180
- key_vectors: bfloat16 [8192, 4096], P('ctx', 'head'), may hold values from -7 to 7
- values: bfloat16 [8192, 4096], P('ctx', 'head'), may hold values from -6 to 6
- kernel: float32 [32, 6, 11], P('head'), may hold values from -0.6 to 0.6
- mixing: float32 [32, 2], P('head'), may hold values from 0.3 to 1
- norm_gain: float32 [4096], P('head'), may hold values from 0.5 to 1.5
- doc_lengths: int32 [8], replicated, may hold values from 1 to 4096, 8192 in all
Outputs:
- attended: bfloat16 [8192, 4096], P('ctx', 'head')
The draws below stay inside these ranges and needn't reach their ends.
Inputs may be any that keep to these rules, and one draw needn't show every extreme that they name: `doc_lengths`: document lengths in order, summing to 8192, the longest exactly 4096.
All inputs are finite; a program needn't handle non-finite values.
Results may differ from the reference program's by a relative error of at most 0.007.
Values may be sent and summed in bfloat16 or wider, within the bound.
No kernel may reach another device: no remote copies, remote signals or barrier semaphores. Data moves between devices by JAX's collectives and lax.ppermute only.
A program may use at most 64 MiB of HBM per device.

```python
import math
import jax
import jax.numpy as jnp
import numpy as np
from jax import lax

HEADS = 32
HEAD_DIM = 128
TOK_DEV = 512
QUERY_TAPS = 6
KEY_TAPS = 11
DOCS = 8
TOKENS = 8192
DOC_MOST = 4096
N_CTX = 16


def draw_pair(key):
    shape = (TOKENS, HEADS * HEAD_DIM)
    key_draw = jnp.clip(jax.random.normal(jax.random.fold_in(key, 101), shape, jnp.float32), -6.0, 6.0)
    query_draw = jnp.clip(jax.random.normal(jax.random.fold_in(key, 102), shape, jnp.float32), -6.0, 6.0)
    return (query_draw, key_draw)


def draw_queries(key, part):
    return draw_pair(key)[0].astype(jnp.bfloat16)


def draw_key_vectors(key, part):
    return draw_pair(key)[1].astype(jnp.bfloat16)


def level_of(stream_key, extent, split, least, largest):
    factor_of = 1.0
    for axis_at, parts in split:
        steps = jax.random.uniform(jax.random.fold_in(jax.random.fold_in(stream_key, 6), axis_at), (parts,), jnp.float32, least / len(split), largest / len(split))
        factor_of = factor_of * jnp.repeat(jnp.exp(steps), extent[axis_at] // parts).reshape((-1,) + (1,) * (len(extent) - 1 - axis_at))
    return factor_of


def profile(amount, total, limit, skew):
    loads = [(1 << 20) // math.isqrt(rank ** skew) + 1 for rank in range(2, amount + 1)]
    spare, counts = total - limit - (amount - 1), [1] * (amount - 1)
    while spare > 0:
        free = [i for i in range(amount - 1) if counts[i] < limit]
        mass, left = sum([loads[i] for i in free]), spare
        for i in free:
            more = min(limit - counts[i], max(1, left * loads[i] // mass), spare)
            counts[i] = counts[i] + more
            spare = spare - more
    return np.array([limit] + counts)


def uneven_parts(key, amount, total, limit, slope):
    if amount == 2:
        one = jax.random.randint(key, (), max(1, total - limit), min(limit, total - 1) + 1)
        return jnp.stack([one, total - one])
    sizes = jnp.asarray(profile(amount, total, limit, slope), jnp.int32)
    couples = (amount - 1) // 2
    donor, receiver = sizes[1:1 + 2 * couples:2], sizes[2:2 + 2 * couples:2]
    margin = jnp.minimum(donor - 1, limit - receiver)
    shifted = jax.random.randint(jax.random.fold_in(key, 1), (couples,), 0, 1 << 20) % (margin + 1)
    sizes = sizes.at[1:1 + 2 * couples:2].set(donor - shifted).at[2:2 + 2 * couples:2].set(receiver + shifted)
    return sizes[jax.random.permutation(jax.random.fold_in(key, 2), amount)]


def bell_draw(rng, dims, scale, most, shards=(), kind=jnp.bfloat16):
    values = jax.random.normal(rng, dims, jnp.float32) * scale
    if len(shards) > 0:
        values = level_of(rng, dims, shards, -0.22, 0.18) * values
    return jnp.clip(values, min=-most, max=most).astype(kind)


def setup_inputs(seed: int = 0) -> dict:
    keys = jax.random.split(jax.random.key(seed), 8)
    return {
        "queries": draw_queries(jax.random.fold_in(keys[7], 71), 0),
        "key_vectors": draw_key_vectors(jax.random.fold_in(keys[7], 71), 0),
        "values": bell_draw(keys[2], (TOKENS, HEADS * HEAD_DIM), 1.0, 6.0, ((0, 16), (1, 32))),
        "kernel": bell_draw(keys[3], (HEADS, QUERY_TAPS, KEY_TAPS), 0.15, 0.6, ((0, 32),), jnp.float32),
        "mixing": jnp.clip(0.3 + 0.7 * jax.random.uniform(keys[4], (HEADS, 2), jnp.float32) ** level_of(keys[4], (HEADS, 2), ((0, 32),), -0.2, 0.2), 0.3, 1.0),
        "norm_gain": jnp.clip(1.0 + 0.1 * jax.random.normal(keys[5], (HEADS * HEAD_DIM,), jnp.float32), 0.5, 1.5),
        "doc_lengths": uneven_parts(keys[6], DOCS, TOKENS, DOC_MOST, 2).astype(jnp.int32),
    }


def doc_ids(positions, doc_ends):
    return lax.optimization_barrier(jnp.sum((positions[:, None] >= doc_ends[None, :]).astype(jnp.int32), axis=1))

def reference(queries, key_vectors, values, kernel, mixing, norm_gain, doc_lengths):
    rim_q = QUERY_TAPS - 1
    rim_k = (KEY_TAPS - 1) // 2
    doc_ends = jnp.cumsum(doc_lengths).astype(jnp.int32)

    def heads_first(matrix):
        return jnp.transpose(matrix.reshape(TOKENS, HEADS, HEAD_DIM), (1, 0, 2))
    query_heads = heads_first(queries)
    key_heads = heads_first(key_vectors)
    value_heads = heads_first(values)
    partner_values = jnp.roll(value_heads, HEADS // 2, axis=0)
    col_pos = jnp.arange(TOKENS + 2 * rim_k, dtype=jnp.int32) - rim_k
    col_doc = doc_ids(col_pos, doc_ends)

    def one_head(operands):
        query_h, key_h, value_h, other_h, taps = operands
        query_pad = jnp.pad(query_h, ((rim_q, 0), (0, 0)))
        key_pad = jnp.pad(key_h, ((rim_k, rim_k), (0, 0)))

        def one_block(block_idx):
            first_row = (block_idx * TOK_DEV).astype(jnp.int32)
            query_ext = lax.dynamic_slice_in_dim(query_pad, first_row, TOK_DEV + rim_q, 0)
            scores = jnp.dot(query_ext, key_pad.T, preferred_element_type=jnp.float32) * HEAD_DIM ** (-0.5)
            row_pos = first_row - rim_q + jnp.arange(TOK_DEV + rim_q, dtype=jnp.int32)
            row_doc = doc_ids(row_pos, doc_ends)
            allowed = (col_pos[None, :] >= 0) & (col_pos[None, :] <= row_pos[:, None]) & (row_doc[:, None] == col_doc[None, :])
            masked = jnp.where(allowed, scores, jnp.float32(0.0))
            conv = masked[rim_q:, rim_k:rim_k + TOKENS]
            for tap_q in range(QUERY_TAPS):
                for tap_k in range(KEY_TAPS):
                    conv = conv + taps[tap_q, tap_k] * masked[rim_q - tap_q:rim_q - tap_q + TOK_DEV, 2 * rim_k - tap_k:2 * rim_k - tap_k + TOKENS]
            logits = jnp.where(allowed[rim_q:, rim_k:rim_k + TOKENS], conv, -jnp.inf)
            top = lax.optimization_barrier(jnp.max(logits, axis=1))
            weights = jnp.exp(logits - top[:, None])
            total = lax.optimization_barrier(jnp.sum(weights, axis=1))
            rounded = weights.astype(jnp.bfloat16)
            own = jnp.dot(rounded, value_h, preferred_element_type=jnp.float32) / total[:, None]
            cross = jnp.dot(rounded, other_h, preferred_element_type=jnp.float32) / total[:, None]
            return (own, cross)
        own, cross = lax.map(one_block, jnp.arange(N_CTX, dtype=jnp.int32))
        return (own.reshape(TOKENS, HEAD_DIM), cross.reshape(TOKENS, HEAD_DIM))
    own, cross = lax.map(one_head, (query_heads, key_heads, value_heads, partner_values, kernel))
    cross_rounded = cross.astype(jnp.bfloat16)
    received = jnp.roll(cross_rounded, HEADS // 2, axis=0).astype(jnp.float32)
    mixed = mixing[:, 0][:, None, None] * own + mixing[:, 1][:, None, None] * received
    normed = mixed * lax.rsqrt(lax.optimization_barrier(jnp.mean(mixed * mixed, axis=2, keepdims=True)) + 1e-05) * norm_gain.reshape(HEADS, 1, HEAD_DIM)
    return jnp.transpose(normed, (1, 0, 2)).reshape(TOKENS, HEADS * HEAD_DIM).astype(jnp.bfloat16)
```

```python
import functools

import jax
import jax.numpy as jnp
from jax import lax
from jax.experimental import pallas as pl
from jax.experimental.pallas import tpu as pltpu
from jax.sharding import PartitionSpec as P

HEAD_DIM = 128
SCALE = HEAD_DIM ** (-0.5)
MASKED = -1e30
FLOOR = -1e20
HALO = 16
BAND = 64
GROUP = 128
WIDE = 256
REACH = 10
HOPS = 4


def dot(a, b):
    return lax.dot_general(a, b, (((1,), (0,)), ((), ())), preferred_element_type=jnp.float32)


def dot_t(a, b):
    return lax.dot_general(a, b, (((1,), (1,)), ((), ())), preferred_element_type=jnp.float32)


def starts_of(position, ends):
    start = jnp.zeros_like(position)
    for end in ends:
        start = jnp.where(position >= end, end, start)
    return start


def widen(column, times):
    return jnp.concatenate([column] * times, axis=1) if times > 1 else column


def absorb(rows, logits, values, m_ref, l_ref, acc_ref):
    m_old = m_ref[rows, :]
    m_new = jnp.maximum(m_old, jnp.max(logits, axis=1, keepdims=True))
    weights = jnp.exp(logits - widen(m_new, logits.shape[1] // 128))
    factor = jnp.exp(m_old - m_new)
    m_ref[rows, :] = m_new
    l_ref[rows, :] = l_ref[rows, :] * factor + jnp.sum(weights, axis=1, keepdims=True)
    acc_ref[rows, :] = acc_ref[rows, :] * widen(factor, 2) + dot(
        weights.astype(jnp.bfloat16), values
    )


def lay_keys(k_ref, vh_ref, kx_ref, vx_ref):
    keys = k_ref.shape[0]
    kx_ref[0:HALO, :] = vh_ref[keys : keys + HALO, 0:HEAD_DIM]
    kx_ref[HALO : HALO + keys, :] = k_ref[...]
    kx_ref[HALO + keys : 2 * HALO + keys, :] = vh_ref[keys : keys + HALO, HEAD_DIM:]
    vx_ref[0:HALO, :] = jnp.zeros((HALO, 2 * HEAD_DIM), jnp.bfloat16)
    vx_ref[HALO : HALO + keys, :] = vh_ref[0:keys, :]
    vx_ref[HALO + keys :, :] = jnp.zeros((HALO, 2 * HEAD_DIM), jnp.bfloat16)


def near(a, chip_row, block, ends, taps_ref, qp_ref, kx_ref, vx_ref, m_ref, l_ref, acc_ref):
    keys = vx_ref.shape[0] - 2 * HALO
    query_taps, key_taps = qp_ref.shape[1] // HEAD_DIM, taps_ref.shape[0] // (qp_ref.shape[1] // HEAD_DIM)
    rim = (key_taps - 1) // 2
    low = pl.multiple_of(jnp.clip(a - 32, 0, keys + 2 * HALO - GROUP), 16)
    rows = pl.ds(pl.multiple_of(block - chip_row + a, 16), BAND)
    window = kx_ref[pl.ds(low, GROUP), :]
    shape = (BAND, GROUP)
    row = block + a + lax.broadcasted_iota(jnp.int32, shape, 0)
    col = block - HALO + low + lax.broadcasted_iota(jnp.int32, shape, 1)
    sums = [None] * key_taps
    own_start = None
    for u in range(query_taps):
        scores = dot_t(qp_ref[rows, u * HEAD_DIM : (u + 1) * HEAD_DIM], window)
        start = starts_of(row - u, ends)
        if u == 0:
            own_start = start
        scores = jnp.where((col <= row - u) & (col >= start), scores, 0.0)
        for t in range(key_taps):
            tap = taps_ref[u * key_taps + t] * SCALE
            if u == 0 and t == rim:
                tap = tap + SCALE
            sums[t] = scores * tap if u == 0 else sums[t] + scores * tap
    conv = sums[rim]
    for t in range(key_taps):
        if t != rim:
            conv = conv + pltpu.roll(sums[t], (t - rim) % GROUP, 1)
    inside = (col >= block) & (col < block + keys)
    inside = inside & (col <= row) & (col > row - REACH) & (col >= own_start)
    logits = jnp.where(inside, conv, MASKED)
    absorb(rows, logits, vx_ref[pl.ds(low, GROUP), :], m_ref, l_ref, acc_ref)


def convolve(local, block, first_start, ends, th_ref, tl_ref, kx_ref, kp_ref):
    total = kx_ref.shape[0]
    keys = kp_ref.shape[0]
    width = kp_ref.shape[1] // 2
    taps = width // HEAD_DIM
    depth = th_ref.shape[1]
    if local:
        for g in range(keys // GROUP):
            shape = (GROUP, depth)
            out = block + g * GROUP + lax.broadcasted_iota(jnp.int32, shape, 0)
            inp = block + g * GROUP - HALO + lax.broadcasted_iota(jnp.int32, shape, 1)
            keep = inp >= starts_of(out, ends)
            window = kx_ref[g * GROUP : g * GROUP + depth, :]
            for u in range(taps):
                part = slice(u * GROUP, (u + 1) * GROUP)
                high = jnp.where(keep, th_ref[part, :].astype(jnp.float32), 0.0).astype(jnp.bfloat16)
                rest = jnp.where(keep, tl_ref[part, :].astype(jnp.float32), 0.0).astype(jnp.bfloat16)
                done = dot(high, window) + dot(rest, window)
                top = done.astype(jnp.bfloat16)
                here = slice(g * GROUP, (g + 1) * GROUP)
                kp_ref[here, u * HEAD_DIM : (u + 1) * HEAD_DIM] = top
                kp_ref[here, width + u * HEAD_DIM : width + (u + 1) * HEAD_DIM] = (
                    done - top.astype(jnp.float32)
                ).astype(jnp.bfloat16)
        return
    place = block - HALO + lax.broadcasted_iota(jnp.int32, (total, HEAD_DIM), 0)
    kx_ref[...] = jnp.where(place >= first_start, kx_ref[...].astype(jnp.float32), 0.0).astype(
        jnp.bfloat16
    )
    for g in range(0, keys // GROUP, 2):
        window = jnp.concatenate(
            [kx_ref[n * GROUP : n * GROUP + depth, :] for n in (g, g + 1)], axis=1
        )
        for u in range(taps):
            part = slice(u * GROUP, (u + 1) * GROUP)
            done = dot(th_ref[part, :], window) + dot(tl_ref[part, :], window)
            top = done.astype(jnp.bfloat16)
            rest = (done - top.astype(jnp.float32)).astype(jnp.bfloat16)
            for n in (0, 1):
                here = slice((g + n) * GROUP, (g + n + 1) * GROUP)
                lanes = slice(n * HEAD_DIM, (n + 1) * HEAD_DIM)
                kp_ref[here, u * HEAD_DIM : (u + 1) * HEAD_DIM] = top[:, lanes]
                kp_ref[here, width + u * HEAD_DIM : width + (u + 1) * HEAD_DIM] = rest[:, lanes]


def far(chip_row, block, ends, qp_ref, kp_ref, vx_ref, m_ref, l_ref, acc_ref):
    keys = kp_ref.shape[0]
    width = qp_ref.shape[1]

    @pl.loop(0, qp_ref.shape[0] // WIDE)
    def _(tile):
        first = tile * WIDE
        top = chip_row + first
        needed = (top + WIDE - 1 >= block + REACH) & (block + keys > starts_of(top, ends))

        @pl.when(needed)
        def _():
            rows = pl.ds(pl.multiple_of(first, WIDE), WIDE)
            query = qp_ref[rows, :]
            conv = dot_t(query, kp_ref[:, 0:width]) + dot_t(query, kp_ref[:, width:])
            shape = (WIDE, GROUP)
            row = top + lax.broadcasted_iota(jnp.int32, shape, 0)
            start = widen(starts_of(row, ends) - block, keys // GROUP)
            row = widen(row - (REACH + block), keys // GROUP)
            col = lax.broadcasted_iota(jnp.int32, (WIDE, keys), 1)
            logits = jnp.where((col <= row) & (col >= start), conv, MASKED)
            absorb(rows, logits, vx_ref[HALO : HALO + keys, :], m_ref, l_ref, acc_ref)


def ends_of(place_ref):
    return [place_ref[2 + d] for d in range(7)]


def local_kernel(
    place_ref, taps_ref, qx_ref, k_ref, vh_ref,
    qp_ref, th_ref, tl_ref, m_ref, l_ref, acc_ref,
    kx_ref, vx_ref, kp_ref,
):
    chip_row, block = place_ref[0], place_ref[1]
    ends = ends_of(place_ref)
    keys = k_ref.shape[0]
    taps = qp_ref.shape[1] // HEAD_DIM
    key_taps = taps_ref.shape[0] // taps
    rim = (key_taps - 1) // 2
    queries = qx_ref[...].astype(jnp.float32)
    for u in range(taps):
        shifted = queries if u == 0 else pltpu.roll(queries, u, 0)
        qp_ref[:, u * HEAD_DIM : (u + 1) * HEAD_DIM] = shifted[HALO:, :].astype(jnp.bfloat16)
    shape = (GROUP, th_ref.shape[1])
    ahead = lax.broadcasted_iota(jnp.int32, shape, 1) - lax.broadcasted_iota(jnp.int32, shape, 0)
    for u in range(taps):
        band = jnp.zeros(shape, jnp.float32)
        for t in range(key_taps):
            tap = taps_ref[u * key_taps + t] * SCALE
            if u == 0 and t == rim:
                tap = tap + SCALE
            band = jnp.where(ahead == HALO + rim - t, tap, band)
        high = band.astype(jnp.bfloat16)
        th_ref[u * GROUP : (u + 1) * GROUP, :] = high
        tl_ref[u * GROUP : (u + 1) * GROUP, :] = (band - high.astype(jnp.float32)).astype(
            jnp.bfloat16
        )
    m_ref[...] = jnp.full(m_ref.shape, FLOOR, jnp.float32)
    l_ref[...] = jnp.zeros(l_ref.shape, jnp.float32)
    acc_ref[...] = jnp.zeros(acc_ref.shape, jnp.float32)
    kx_ref[...] = jnp.zeros(kx_ref.shape, jnp.bfloat16)
    lay_keys(k_ref, vh_ref, kx_ref, vx_ref)

    @pl.loop(0, keys // BAND + 1)
    def _(tile):
        a = tile * BAND

        @pl.when(block - chip_row + a < qp_ref.shape[0])
        def _():
            near(
                a, chip_row, block, ends, taps_ref, qp_ref, kx_ref, vx_ref, m_ref, l_ref, acc_ref
            )

    convolve(True, block, 0, ends, th_ref, tl_ref, kx_ref, kp_ref)
    far(chip_row, block, ends, qp_ref, kp_ref, vx_ref, m_ref, l_ref, acc_ref)


def hop_kernel(
    last, place_ref, taps_ref, qp_ref, th_ref, tl_ref, k_ref, vh_ref, m_in, l_in, acc_in, *rest
):
    if last:
        keep_ref, send_ref, kx_ref, vx_ref, kp_ref, m_ref, l_ref, acc_ref = rest
    else:
        m_ref, l_ref, acc_ref, kx_ref, vx_ref, kp_ref = rest
    chip_row, block = place_ref[0], place_ref[1]
    ends = ends_of(place_ref)
    keys = k_ref.shape[0]
    first_start = starts_of(chip_row, ends)
    m_ref[...] = m_in[...]
    l_ref[...] = l_in[...]
    acc_ref[...] = acc_in[...]

    @pl.when(block + keys > first_start)
    def _():
        kx_ref[...] = jnp.zeros(kx_ref.shape, jnp.bfloat16)
        lay_keys(k_ref, vh_ref, kx_ref, vx_ref)

        @pl.when(block + keys == chip_row)
        def _():
            near(
                keys, chip_row, block, ends, taps_ref, qp_ref, kx_ref, vx_ref, m_ref, l_ref, acc_ref
            )

        convolve(False, block, first_start, ends, th_ref, tl_ref, kx_ref, kp_ref)
        far(chip_row, block, ends, qp_ref, kp_ref, vx_ref, m_ref, l_ref, acc_ref)

    if last:
        core = place_ref[9]
        lane = lax.broadcasted_iota(jnp.int32, (keys, 128), 1)
        for ref, side in ((keep_ref, core), (send_ref, 1 - core)):
            rows = pl.ds(pl.multiple_of(side * keys, keys), keys)
            ref[:, 0 : 2 * HEAD_DIM] = acc_ref[rows, :]
            ref[:, 2 * HEAD_DIM :] = jnp.where(lane < 64, m_ref[rows, :], l_ref[rows, :])


def join_kernel(keep_ref, other_ref, own_ref, cross_ref):
    wide = 2 * HEAD_DIM
    stats, more = keep_ref[:, wide:], other_ref[:, wide:]
    m_a, l_a = stats[:, 0:1], stats[:, 64:65]
    m_b, l_b = more[:, 0:1], more[:, 64:65]
    m = jnp.maximum(m_a, m_b)
    f_a, f_b = jnp.exp(m_a - m), jnp.exp(m_b - m)
    share = 1.0 / (l_a * f_a + l_b * f_b)
    f_a, f_b = f_a * share, f_b * share
    own_ref[...] = keep_ref[:, :HEAD_DIM] * f_a + other_ref[:, :HEAD_DIM] * f_b
    cross_ref[...] = (
        keep_ref[:, HEAD_DIM:wide] * f_a + other_ref[:, HEAD_DIM:wide] * f_b
    ).astype(jnp.bfloat16)


def finish_kernel(mixing_ref, own_ref, cross_ref, gain_ref, out_ref):
    mixed = mixing_ref[0] * own_ref[...] + mixing_ref[1] * cross_ref[...].astype(jnp.float32)
    mean = jnp.mean(mixed * mixed, axis=1, keepdims=True)
    out_ref[...] = (mixed * lax.rsqrt(mean + 1e-05) * gain_ref[...]).astype(jnp.bfloat16)


VMEM = pl.BlockSpec(memory_space=pltpu.VMEM)
SMEM = pl.BlockSpec(memory_space=pltpu.SMEM)


def call(kernel, specs, out, scratch, args, aliases=None, flops=0):
    shapes = [jax.ShapeDtypeStruct(shape, dtype) for shape, dtype in out]
    return pl.pallas_call(
        kernel,
        out_shape=shapes,
        in_specs=specs,
        out_specs=[VMEM] * len(shapes),
        scratch_shapes=scratch,
        input_output_aliases=aliases or {},
        cost_estimate=pl.CostEstimate(flops=flops, bytes_accessed=4 << 20, transcendentals=0),
        compiler_params=pltpu.CompilerParams(vmem_limit_bytes=40 << 20),
    )(*args)


def body(queries, key_vectors, values, kernel, mixing, norm_gain, doc_lengths):
    rows = queries.shape[0]
    bf16, f32 = jnp.bfloat16, jnp.float32
    count = lax.axis_size("ctx")
    heads = lax.axis_size("head")
    group = lax.axis_index("ctx")
    core = group % 2
    taps = kernel.shape[1]
    width = taps * HEAD_DIM

    def permute(value, pairs):
        return lax.ppermute(value, "ctx", pairs)

    def onward(value):
        return permute(value, [(i, (i + 2) % count) for i in range(count)])

    def partner(value):
        return lax.ppermute(value, "head", [(i, i ^ (heads // 2)) for i in range(heads)])

    across = [(2 * i + 1, (2 * i + 2) % count) for i in range(count // 2)]
    across = across + [(b, a) for a, b in across]
    edge = permute(
        jnp.concatenate([key_vectors[:HALO], key_vectors[rows - HALO :], queries[rows - HALO :]]),
        across,
    )
    other_values = partner(values)
    sibling = permute(
        jnp.concatenate(
            [queries, key_vectors[:HALO], key_vectors[rows - HALO :], edge[2 * HALO :]]
        ),
        [(i, i ^ 1) for i in range(count)],
    )
    even = core == 0
    behind = jnp.where(even, edge[HALO : 2 * HALO], sibling[rows + HALO : rows + 2 * HALO])
    beyond = jnp.where(even, sibling[rows : rows + HALO], edge[:HALO])
    query_ext = jnp.where(
        even,
        jnp.concatenate([edge[2 * HALO :], queries, sibling[:rows]]),
        jnp.concatenate([sibling[rows + 2 * HALO :], sibling[:rows], queries]),
    )
    pairs = jnp.concatenate(
        [
            jnp.concatenate([values, other_values], axis=1),
            jnp.concatenate([behind, beyond], axis=1),
        ]
    )
    doc_ends = jnp.cumsum(doc_lengths)[:7]
    chip = group // 2

    def place(hop):
        head = jnp.stack([chip * 2 * rows, (chip - hop) * 2 * rows + core * rows])
        return jnp.concatenate([head, doc_ends, core[None]]).astype(jnp.int32)

    flat = kernel.reshape(-1)
    state = [((2 * rows, 128), f32), ((2 * rows, 128), f32), ((2 * rows, 2 * HEAD_DIM), f32)]
    scratch = [
        pltpu.VMEM((rows + 128, HEAD_DIM), bf16),
        pltpu.VMEM((rows + 2 * HALO, 2 * HEAD_DIM), bf16),
        pltpu.VMEM((rows, 2 * width), bf16),
    ]
    keys = key_vectors
    flops = 2 * 2 * rows * rows * (2 * width + 2 * HEAD_DIM)
    qp, high, low, m, l, acc = call(
        local_kernel,
        [SMEM, SMEM, VMEM, VMEM, VMEM],
        [((2 * rows, width), bf16), ((taps * GROUP, 256), bf16), ((taps * GROUP, 256), bf16)]
        + state,
        scratch,
        (place(0), flat, query_ext, keys, pairs),
        flops=flops,
    )
    for hop in range(1, HOPS + 1):
        keys, pairs = onward(keys), onward(pairs)
        last = hop == HOPS
        out = [((rows, 3 * HEAD_DIM), f32)] * 2 if last else state
        extra = [pltpu.VMEM(shape, dtype) for shape, dtype in state] if last else []
        result = call(
            functools.partial(hop_kernel, last),
            [SMEM, SMEM] + [VMEM] * 8,
            out,
            scratch + extra,
            (place(hop), flat, qp, high, low, keys, pairs, m, l, acc),
            aliases=None if last else {7: 0, 8: 1, 9: 2},
            flops=flops,
        )
        if not last:
            m, l, acc = result
    keep, send = result
    other = permute(send, [(i, i ^ 1) for i in range(count)])
    own, cross = call(
        join_kernel,
        [VMEM, VMEM],
        [((rows, HEAD_DIM), f32), ((rows, HEAD_DIM), bf16)],
        [],
        (keep, other),
    )
    (finished,) = call(
        finish_kernel,
        [SMEM, VMEM, VMEM, VMEM],
        [((rows, HEAD_DIM), bf16)],
        [],
        (mixing.reshape(-1), own, partner(cross), norm_gain.reshape(1, HEAD_DIM)),
    )
    return finished


def solution(mesh):
    return jax.shard_map(
        body,
        mesh=mesh,
        in_specs=(
            P("ctx", "head"),
            P("ctx", "head"),
            P("ctx", "head"),
            P("head", None, None),
            P("head", None),
            P("head"),
            P(),
        ),
        out_specs=P("ctx", "head"),
        check_vma=False,
    )
```

```python
import functools

import jax
import jax.numpy as jnp
from jax import lax
from jax.experimental import pallas as pl
from jax.experimental.pallas import tpu as pltpu
from jax.sharding import PartitionSpec as P

HEAD_DIM = 128
SCALE = HEAD_DIM ** (-0.5)
MASKED = -1e30
FLOOR = -1e20
HALO = 16
BAND = 64
GROUP = 128
WIDE = 256
REACH = 10
HOPS = 4


def dot(a, b):
    return lax.dot_general(a, b, (((1,), (0,)), ((), ())), preferred_element_type=jnp.float32)


def dot_t(a, b):
    return lax.dot_general(a, b, (((1,), (1,)), ((), ())), preferred_element_type=jnp.float32)


def starts_of(position, ends):
    start = jnp.zeros_like(position)
    for end in ends:
        start = jnp.where(position >= end, end, start)
    return start


def widen(column, times):
    return jnp.concatenate([column] * times, axis=1) if times > 1 else column


def absorb(tiles, state_ref):
    wide = 2 * HEAD_DIM
    done = []
    for rows, logits, values in tiles:
        m_old = state_ref[rows, wide : wide + 128]
        m_new = jnp.maximum(m_old, jnp.max(logits, axis=1, keepdims=True))
        weights = jnp.exp(logits - widen(m_new, logits.shape[1] // 128))
        factor = jnp.exp(m_old - m_new)
        total = state_ref[rows, wide + 128 :] * factor + jnp.sum(weights, axis=1, keepdims=True)
        product = dot(weights.astype(jnp.bfloat16), values)
        product = state_ref[rows, 0:wide] * widen(factor, 2) + product
        done.append((rows, m_new, total, product))
    for rows, m_new, total, product in done:
        state_ref[rows, 0:wide] = product
        state_ref[rows, wide : wide + 128] = m_new
        state_ref[rows, wide + 128 :] = total


def taps_at(qp_ref, rest, u):
    most = qp_ref.shape[1] // 256
    sets = qp_ref.shape[1] // HEAD_DIM // most
    row = qp_ref.shape[0] - (2 - rest) * sets * GROUP + u // most * GROUP
    return slice(row, row + GROUP), slice(u % most * 256, u % most * 256 + 256)


def lay_keys(a_ref, b_ref, kx_ref, vx_ref):
    keys = vx_ref.shape[0] - 2 * HALO
    own = a_ref.shape[0] - keys - 2 * HALO
    kx_ref[0:HALO, :] = a_ref[keys : keys + HALO, :]
    kx_ref[HALO : HALO + keys, :] = a_ref[0:keys, :]
    kx_ref[HALO + keys : 2 * HALO + keys, :] = a_ref[keys + HALO : keys + 2 * HALO, :]
    vx_ref[0:HALO, :] = jnp.zeros((HALO, 2 * HEAD_DIM), jnp.bfloat16)
    vx_ref[HALO : HALO + own, 0:HEAD_DIM] = a_ref[keys + 2 * HALO :, :]
    vx_ref[HALO + own : HALO + keys, 0:HEAD_DIM] = b_ref[0 : keys - own, :]
    vx_ref[HALO : HALO + keys, HEAD_DIM:] = b_ref[keys - own :, :]
    vx_ref[HALO + keys :, :] = jnp.zeros((HALO, 2 * HEAD_DIM), jnp.bfloat16)


def near(a, chip_row, block, ends, taps_ref, qp_ref, kx_ref, vx_ref, state_ref):
    keys = vx_ref.shape[0] - 2 * HALO
    query_taps, key_taps = taps_ref.shape[1:]
    rim = (key_taps - 1) // 2
    low = pl.multiple_of(jnp.clip(a - 32, 0, keys + 2 * HALO - GROUP), 16)
    rows = pl.ds(pl.multiple_of(block - chip_row + a, 16), BAND)
    window = kx_ref[pl.ds(low, GROUP), :]
    shape = (BAND, GROUP)
    row = block + a + lax.broadcasted_iota(jnp.int32, shape, 0)
    col = block - HALO + low + lax.broadcasted_iota(jnp.int32, shape, 1)
    sums = [None] * key_taps
    own_start = None
    for u in range(query_taps):
        scores = dot_t(qp_ref[rows, u * HEAD_DIM : (u + 1) * HEAD_DIM], window)
        start = starts_of(row - u, ends)
        if u == 0:
            own_start = start
        scores = jnp.where((col <= row - u) & (col >= start), scores, 0.0)
        for t in range(key_taps):
            tap = taps_ref[0, u, t] * SCALE
            if u == 0 and t == rim:
                tap = tap + SCALE
            sums[t] = scores * tap if u == 0 else sums[t] + scores * tap
    conv = sums[rim]
    for t in range(key_taps):
        if t != rim:
            conv = conv + pltpu.roll(sums[t], (t - rim) % GROUP, 1)
    inside = (col >= block) & (col < block + keys)
    inside = inside & (col <= row) & (col > row - REACH) & (col >= own_start)
    logits = jnp.where(inside, conv, MASKED)
    absorb([(rows, logits, vx_ref[pl.ds(low, GROUP), :])], state_ref)


def convolve(local, block, first_start, ends, qp_ref, kx_ref, kp_ref):
    total = kx_ref.shape[0]
    keys = kp_ref.shape[0]
    width = kp_ref.shape[1] // 2
    taps = width // HEAD_DIM
    depth = 256
    def put(g, u, done):
        top = done.astype(jnp.bfloat16)
        rest = (done - top.astype(jnp.float32)).astype(jnp.bfloat16)
        for n in range(done.shape[1] // HEAD_DIM):
            here = slice((g + n) * GROUP, (g + n + 1) * GROUP)
            lanes = slice(n * HEAD_DIM, (n + 1) * HEAD_DIM)
            kp_ref[here, u * HEAD_DIM : (u + 1) * HEAD_DIM] = top[:, lanes]
            kp_ref[here, width + u * HEAD_DIM : width + (u + 1) * HEAD_DIM] = rest[:, lanes]

    def whole():
        for g in range(0, keys // GROUP, 2):
            window = jnp.concatenate(
                [kx_ref[n * GROUP : n * GROUP + depth, :] for n in (g, g + 1)], axis=1
            )
            for u in range(taps):
                high, rest = (qp_ref[taps_at(qp_ref, n, u)] for n in (0, 1))
                put(g, u, dot(high, window) + dot(rest, window))

    def cut():
        for g in range(keys // GROUP):
            shape = (GROUP, depth)
            out = block + g * GROUP + lax.broadcasted_iota(jnp.int32, shape, 0)
            inp = block + g * GROUP - HALO + lax.broadcasted_iota(jnp.int32, shape, 1)
            keep = inp >= starts_of(out, ends)
            window = kx_ref[g * GROUP : g * GROUP + depth, :]
            for u in range(taps):
                high, rest = (
                    jnp.where(keep, qp_ref[taps_at(qp_ref, n, u)].astype(jnp.float32), 0.0).astype(
                        jnp.bfloat16
                    )
                    for n in (0, 1)
                )
                put(g, u, dot(high, window) + dot(rest, window))

    if local:
        unbroken = starts_of(block + keys - 1, ends) <= block - HALO

        @pl.when(unbroken)
        def _():
            whole()

        @pl.when(jnp.logical_not(unbroken))
        def _():
            cut()

        return
    place = block - HALO + lax.broadcasted_iota(jnp.int32, (total, HEAD_DIM), 0)
    kx_ref[...] = jnp.where(place >= first_start, kx_ref[...].astype(jnp.float32), 0.0).astype(
        jnp.bfloat16
    )
    whole()


def far(chip_row, block, ends, qp_ref, kp_ref, vx_ref, state_ref):
    keys = kp_ref.shape[0]
    width = qp_ref.shape[1]

    @pl.loop(0, state_ref.shape[0] // (2 * WIDE))
    def _(tile):
        first = tile * 2 * WIDE
        top = chip_row + first
        needed = (top + 2 * WIDE - 1 >= block + REACH) & (block + keys > starts_of(top, ends))

        @pl.when(needed)
        def _():
            tiles = []
            shape = (WIDE, GROUP)
            col = lax.broadcasted_iota(jnp.int32, (WIDE, keys), 1)
            for half in (0, WIDE):
                rows = pl.ds(pl.multiple_of(first + half, WIDE), WIDE)
                query = qp_ref[rows, :]
                conv = dot_t(query, kp_ref[:, 0:width]) + dot_t(query, kp_ref[:, width:])
                row = top + half + lax.broadcasted_iota(jnp.int32, shape, 0)
                start = widen(starts_of(row, ends) - block, keys // GROUP)
                row = widen(row - (REACH + block), keys // GROUP)
                logits = jnp.where((col <= row) & (col >= start), conv, MASKED)
                tiles.append((rows, logits, vx_ref[HALO : HALO + keys, :]))
            absorb(tiles, state_ref)


def ends_of(place_ref):
    ends = [place_ref[2]]
    for d in range(1, 7):
        ends.append(ends[-1] + place_ref[2 + d])
    return ends


def local_kernel(
    place_ref, taps_ref, qx_ref, a_ref, b_ref,
    qp_ref, state_ref, done_ref,
    kx_ref, vx_ref, kp_ref,
):
    chip_row, block = place_ref[0], place_ref[1]
    ends = ends_of(place_ref)
    keys = kp_ref.shape[0]
    taps, key_taps = taps_ref.shape[1:]
    rim = (key_taps - 1) // 2
    queries = qx_ref[...].astype(jnp.float32)
    for u in range(taps):
        shifted = queries if u == 0 else pltpu.roll(queries, u, 0)
        qp_ref[0 : state_ref.shape[0], u * HEAD_DIM : (u + 1) * HEAD_DIM] = shifted[
            HALO:, :
        ].astype(jnp.bfloat16)
    shape = (GROUP, 256)
    ahead = lax.broadcasted_iota(jnp.int32, shape, 1) - lax.broadcasted_iota(jnp.int32, shape, 0)
    for u in range(taps):
        band = jnp.zeros(shape, jnp.float32)
        for t in range(key_taps):
            tap = taps_ref[0, u, t] * SCALE
            if u == 0 and t == rim:
                tap = tap + SCALE
            band = jnp.where(ahead == HALO + rim - t, tap, band)
        high = band.astype(jnp.bfloat16)
        qp_ref[taps_at(qp_ref, 0, u)] = high
        qp_ref[taps_at(qp_ref, 1, u)] = (band - high.astype(jnp.float32)).astype(jnp.bfloat16)
    done_ref[...] = jnp.zeros(done_ref.shape, jnp.float32)
    lane = lax.broadcasted_iota(jnp.int32, state_ref.shape, 1)
    floor = (lane >= 2 * HEAD_DIM) & (lane < 2 * HEAD_DIM + 128)
    state_ref[...] = jnp.where(floor, FLOOR, 0.0)
    kx_ref[...] = jnp.zeros(kx_ref.shape, jnp.bfloat16)
    lay_keys(a_ref, b_ref, kx_ref, vx_ref)

    @pl.loop(0, keys // BAND + 1)
    def _(tile):
        a = tile * BAND

        @pl.when(block - chip_row + a < state_ref.shape[0])
        def _():
            near(
                a, chip_row, block, ends, taps_ref, qp_ref, kx_ref, vx_ref, state_ref
            )

    convolve(True, block, 0, ends, qp_ref, kx_ref, kp_ref)
    far(chip_row, block, ends, qp_ref, kp_ref, vx_ref, state_ref)


def hop_kernel(
    last, place_ref, taps_ref, qp_ref, a_ref, b_ref, state_in, *rest
):
    if last:
        keep_ref, send_ref, kx_ref, vx_ref, kp_ref, state_ref = rest
    else:
        state_ref, done_ref, kx_ref, vx_ref, kp_ref = rest
        done_ref[...] = jnp.zeros(done_ref.shape, jnp.float32)
    chip_row, block = place_ref[0], place_ref[1]
    ends = ends_of(place_ref)
    keys = kp_ref.shape[0]
    first_start = starts_of(chip_row, ends)
    state_ref[...] = state_in[...]

    @pl.when(block + keys > first_start)
    def _():
        kx_ref[...] = jnp.zeros(kx_ref.shape, jnp.bfloat16)
        lay_keys(a_ref, b_ref, kx_ref, vx_ref)

        @pl.when(block + keys == chip_row)
        def _():
            near(
                keys, chip_row, block, ends, taps_ref, qp_ref, kx_ref, vx_ref, state_ref
            )

        convolve(False, block, first_start, ends, qp_ref, kx_ref, kp_ref)
        far(chip_row, block, ends, qp_ref, kp_ref, vx_ref, state_ref)

    if last:
        core = place_ref[9]
        lane = lax.broadcasted_iota(jnp.int32, (keys, 128), 1)
        for ref, side in ((keep_ref, core), (send_ref, 1 - core)):
            rows = pl.ds(pl.multiple_of(side * keys, keys), keys)
            wide = 2 * HEAD_DIM
            ref[:, 0:wide] = state_ref[rows, 0:wide]
            ref[:, wide:] = jnp.where(
                lane < 64, state_ref[rows, wide : wide + 128], state_ref[rows, wide + 128 :]
            )


def join_kernel(keep_ref, other_ref, own_ref, cross_ref):
    wide = 2 * HEAD_DIM
    stats, more = keep_ref[:, wide:], other_ref[:, wide:]
    m_a, l_a = stats[:, 0:1], stats[:, 64:65]
    m_b, l_b = more[:, 0:1], more[:, 64:65]
    m = jnp.maximum(m_a, m_b)
    f_a, f_b = jnp.exp(m_a - m), jnp.exp(m_b - m)
    share = 1.0 / (l_a * f_a + l_b * f_b)
    f_a, f_b = f_a * share, f_b * share
    own_ref[...] = keep_ref[:, :HEAD_DIM] * f_a + other_ref[:, :HEAD_DIM] * f_b
    cross_ref[...] = (
        keep_ref[:, HEAD_DIM:wide] * f_a + other_ref[:, HEAD_DIM:wide] * f_b
    ).astype(jnp.bfloat16)


def finish_kernel(mixing_ref, own_ref, cross_ref, gain_ref, out_ref):
    mixed = mixing_ref[0] * own_ref[...] + mixing_ref[1] * cross_ref[...].astype(jnp.float32)
    mean = jnp.mean(mixed * mixed, axis=1, keepdims=True)
    out_ref[...] = (mixed * lax.rsqrt(mean + 1e-05) * gain_ref[...]).astype(jnp.bfloat16)


VMEM = pl.BlockSpec(memory_space=pltpu.VMEM)
SMEM = pl.BlockSpec(memory_space=pltpu.SMEM)


def call(kernel, specs, out, scratch, args, aliases=None, flops=0):
    shapes = [jax.ShapeDtypeStruct(shape, dtype) for shape, dtype in out]
    return pl.pallas_call(
        kernel,
        out_shape=shapes,
        in_specs=specs,
        out_specs=[VMEM] * len(shapes),
        scratch_shapes=scratch,
        input_output_aliases=aliases or {},
        cost_estimate=pl.CostEstimate(flops=flops, bytes_accessed=4 << 20, transcendentals=0),
        compiler_params=pltpu.CompilerParams(vmem_limit_bytes=20 << 20),
    )(*args)


def body(queries, key_vectors, values, kernel, mixing, norm_gain, doc_lengths):
    rows = queries.shape[0]
    bf16, f32 = jnp.bfloat16, jnp.float32
    count = lax.axis_size("ctx")
    heads = lax.axis_size("head")
    group = lax.axis_index("ctx")
    core = group % 2
    taps = kernel.shape[1]
    width = taps * HEAD_DIM

    def permute(value, pairs):
        return lax.ppermute(value, "ctx", pairs)

    def onward(value):
        return permute(value, [(i, (i + 2) % count) for i in range(count)])

    def partner(value):
        return lax.ppermute(value, "head", [(i, i ^ (heads // 2)) for i in range(heads)])

    def step(value, by):
        return permute(value, [(i, (i + by) % count) for i in range(count)])

    other_values = partner(values)
    beyond = step(key_vectors[:HALO], -1)
    behind = step(jnp.concatenate([key_vectors[rows - HALO :], queries[rows - HALO :]]), 1)
    sibling = permute(
        jnp.concatenate([queries, behind[HALO:]]), [(i, i ^ 1) for i in range(count)]
    )
    query_ext = jnp.where(
        core == 0,
        jnp.concatenate([behind[HALO:], queries, sibling[:rows]]),
        jnp.concatenate([sibling[rows:], sibling[:rows], queries]),
    )
    own = (rows - 2 * HALO) // 2
    ring_a = jnp.concatenate([key_vectors, behind[:HALO], beyond, values[:own]])
    ring_b = jnp.concatenate([values[own:], other_values])
    chip = group // 2

    def place(hop):
        head = jnp.stack([chip * 2 * rows, (chip - hop) * 2 * rows + core * rows])
        return jnp.concatenate([head, doc_lengths[:7], core[None]]).astype(jnp.int32)

    state = [((2 * rows, 2 * HEAD_DIM + 256), f32)]
    mark = [((8, 128), f32)]
    scratch = [
        pltpu.VMEM((rows + 128, HEAD_DIM), bf16),
        pltpu.VMEM((rows + 2 * HALO, 2 * HEAD_DIM), bf16),
        pltpu.VMEM((rows, 2 * width), bf16),
    ]
    flops = 2 * 2 * rows * rows * (2 * width + 2 * HEAD_DIM)
    operand, running, done = call(
        local_kernel,
        [SMEM, SMEM, VMEM, VMEM, VMEM],
        [((2 * rows + 2 * taps * GROUP * 256 // width, width), bf16)]
        + state
        + mark,
        scratch,
        (place(0), kernel, query_ext, ring_a, ring_b),
        flops=flops,
    )
    for hop in range(1, HOPS + 1):
        ring_a, ring_b = onward(ring_a), onward(ring_b)
        ring_a, _ = lax.optimization_barrier((ring_a, done))
        ring_b, _ = lax.optimization_barrier((ring_b, done))
        last = hop == HOPS
        out = [((rows, 3 * HEAD_DIM), f32)] * 2 if last else state + mark
        extra = [pltpu.VMEM(shape, dtype) for shape, dtype in state] if last else []
        result = call(
            functools.partial(hop_kernel, last),
            [SMEM, SMEM] + [VMEM] * 4,
            out,
            scratch + extra,
            (place(hop), kernel, operand, ring_a, ring_b, running),
            aliases=None if last else {5: 0},
            flops=flops,
        )
        if not last:
            running, done = result
    keep, send = result
    other = permute(send, [(i, i ^ 1) for i in range(count)])
    own, cross = call(
        join_kernel,
        [VMEM, VMEM],
        [((rows, HEAD_DIM), f32), ((rows, HEAD_DIM), bf16)],
        [],
        (keep, other),
    )
    (finished,) = call(
        finish_kernel,
        [SMEM, VMEM, VMEM, VMEM],
        [((rows, HEAD_DIM), bf16)],
        [],
        (mixing.reshape(-1), own, partner(cross), norm_gain.reshape(1, HEAD_DIM)),
    )
    return finished


def solution(mesh):
    return jax.shard_map(
        body,
        mesh=mesh,
        in_specs=(
            P("ctx", "head"),
            P("ctx", "head"),
            P("ctx", "head"),
            P("head", None, None),
            P("head", None),
            P("head"),
            P(),
        ),
        out_specs=P("ctx", "head"),
        check_vma=False,
    )
```

```python
import functools

import jax
import jax.numpy as jnp
from jax import lax
from jax.experimental import pallas as pl
from jax.experimental.pallas import tpu as pltpu
from jax.sharding import PartitionSpec as P

HEAD_DIM = 128
SCALE = HEAD_DIM ** (-0.5)
MASKED = -1e30
FLOOR = -1e20
HALO = 16
BAND = 64
GROUP = 128
WIDE = 256
REACH = 10
HOPS = 4


def dot(a, b):
    return lax.dot_general(a, b, (((1,), (0,)), ((), ())), preferred_element_type=jnp.float32)


def dot_t(a, b):
    return lax.dot_general(a, b, (((1,), (1,)), ((), ())), preferred_element_type=jnp.float32)


def starts_of(position, ends):
    start = jnp.zeros_like(position)
    for end in ends:
        start = jnp.where(position >= end, end, start)
    return start


def widen(column, times):
    return jnp.concatenate([column] * times, axis=1) if times > 1 else column


def absorb(tiles, source_ref, state_ref):
    wide = 2 * HEAD_DIM
    done = []
    for rows, logits, values in tiles:
        m_old = source_ref[rows, wide : wide + 1]
        m_new = jnp.maximum(m_old, jnp.max(logits, axis=1, keepdims=True))
        weights = jnp.exp(logits - m_new)
        factor = jnp.exp(m_old - m_new)
        total = source_ref[rows, wide + 64 : wide + 65] * factor
        total = total + jnp.sum(weights, axis=1, keepdims=True)
        product = dot(weights.astype(jnp.bfloat16), values)
        product = source_ref[rows, 0:wide] * factor + product
        lane = lax.broadcasted_iota(jnp.int32, (logits.shape[0], 128), 1)
        done.append((rows, jnp.where(lane < 64, m_new, total), product))
    for rows, stats, product in done:
        state_ref[rows, 0:wide] = product
        state_ref[rows, wide:] = stats


def taps_at(qp_ref, rest, u):
    most = qp_ref.shape[1] // 256
    sets = qp_ref.shape[1] // HEAD_DIM // most
    row = qp_ref.shape[0] - (2 - rest) * sets * GROUP + u // most * GROUP
    return slice(row, row + GROUP), slice(u % most * 256, u % most * 256 + 256)


def lay_keys(a_ref, b_ref, kx_ref, vx_ref):
    keys = b_ref.shape[0] // 2
    kx_ref[0:HALO, :] = a_ref[keys : keys + HALO, :]
    kx_ref[HALO : HALO + keys, :] = a_ref[0:keys, :]
    kx_ref[HALO + keys : 2 * HALO + keys, :] = a_ref[keys + HALO : keys + 2 * HALO, :]
    kx_ref[2 * HALO + keys :, :] = jnp.zeros_like(kx_ref[2 * HALO + keys :, :])
    vx_ref[0:HALO, :] = jnp.zeros((HALO, 2 * HEAD_DIM), jnp.bfloat16)
    vx_ref[HALO : HALO + keys, 0:HEAD_DIM] = b_ref[0:keys, :]
    vx_ref[HALO : HALO + keys, HEAD_DIM:] = b_ref[keys:, :]
    vx_ref[HALO + keys :, :] = jnp.zeros((HALO, 2 * HEAD_DIM), jnp.bfloat16)


def near(a, chip_row, block, ends, taps_ref, qp_ref, kx_ref, vx_ref, start_ref, state_ref):
    keys = vx_ref.shape[0] - 2 * HALO
    query_taps, key_taps = taps_ref.shape[1:]
    rim = (key_taps - 1) // 2
    low = pl.multiple_of(jnp.clip(a - 32, 0, keys + 2 * HALO - GROUP), 16)
    rows = pl.ds(pl.multiple_of(block - chip_row + a, 16), BAND)
    window = kx_ref[pl.ds(low, GROUP), :]
    shape = (BAND, GROUP)
    top = block + a
    one_start = starts_of(top + BAND - 1, ends)
    one = starts_of(top - 8, ends) == one_start

    @pl.when(one)
    def _():
        start_ref[...] = jnp.full(start_ref.shape, one_start, jnp.int32)

    @pl.when(jnp.logical_not(one))
    def _():
        position = top - 8 + lax.broadcasted_iota(jnp.int32, start_ref.shape, 0)
        start_ref[...] = starts_of(position, ends)

    row = top + lax.broadcasted_iota(jnp.int32, shape, 0)
    col = block - HALO + low + lax.broadcasted_iota(jnp.int32, shape, 1)
    behind = row - col
    stacked = jnp.concatenate(
        [qp_ref[rows, u * HEAD_DIM : (u + 1) * HEAD_DIM] for u in range(query_taps)], axis=0
    )
    products = dot_t(stacked, window)
    scores = []
    for u in range(query_taps):
        allowed = (behind >= u) & (col >= start_ref[8 - u : 8 - u + BAND, :])
        scores.append(jnp.where(allowed, products[u * BAND : (u + 1) * BAND, :], 0.0))
    conv = None
    for t in range(key_taps):
        terms = None
        for u in range(query_taps):
            tap = taps_ref[0, u, t] * SCALE
            if u == 0 and t == rim:
                tap = tap + SCALE
            terms = scores[u] * tap if terms is None else terms + scores[u] * tap
        if t != rim:
            terms = pltpu.roll(terms, (t - rim) % GROUP, 1)
        conv = terms if conv is None else conv + terms
    inside = (col >= block) & (col < block + keys) & (col >= start_ref[8 : 8 + BAND, :])
    logits = jnp.where(inside & (behind >= 0) & (behind < REACH), conv, MASKED)
    absorb([(rows, logits, vx_ref[pl.ds(low, GROUP), :])], state_ref, state_ref)


def convolve(local, block, first_start, ends, qp_ref, kx_ref, kp_ref):
    total = kx_ref.shape[0]
    keys = kp_ref.shape[0]
    width = kp_ref.shape[1] // 2
    taps = width // HEAD_DIM
    depth = 256
    def put(g, u, done):
        top = done.astype(jnp.bfloat16)
        rest = (done - top.astype(jnp.float32)).astype(jnp.bfloat16)
        for n in range(done.shape[1] // HEAD_DIM):
            here = slice((g + n) * GROUP, (g + n + 1) * GROUP)
            lanes = slice(n * HEAD_DIM, (n + 1) * HEAD_DIM)
            kp_ref[here, u * HEAD_DIM : (u + 1) * HEAD_DIM] = top[:, lanes]
            kp_ref[here, width + u * HEAD_DIM : width + (u + 1) * HEAD_DIM] = rest[:, lanes]

    def whole():
        for g in range(0, keys // GROUP, 2):
            window = jnp.concatenate(
                [kx_ref[n * GROUP : n * GROUP + depth, :] for n in (g, g + 1)], axis=1
            )
            for u in range(taps):
                high, rest = (qp_ref[taps_at(qp_ref, n, u)] for n in (0, 1))
                put(g, u, dot(high, window) + dot(rest, window))

    def cut():
        for g in range(keys // GROUP):
            shape = (GROUP, depth)
            out = block + g * GROUP + lax.broadcasted_iota(jnp.int32, shape, 0)
            inp = block + g * GROUP - HALO + lax.broadcasted_iota(jnp.int32, shape, 1)
            keep = inp >= starts_of(out, ends)
            window = kx_ref[g * GROUP : g * GROUP + depth, :]
            for u in range(taps):
                high, rest = (
                    jnp.where(keep, qp_ref[taps_at(qp_ref, n, u)].astype(jnp.float32), 0.0).astype(
                        jnp.bfloat16
                    )
                    for n in (0, 1)
                )
                put(g, u, dot(high, window) + dot(rest, window))

    if local:
        unbroken = starts_of(block + keys - 1, ends) <= block - HALO

        @pl.when(unbroken)
        def _():
            whole()

        @pl.when(jnp.logical_not(unbroken))
        def _():
            cut()

        return
    place = block - HALO + lax.broadcasted_iota(jnp.int32, (total, HEAD_DIM), 0)
    kx_ref[...] = jnp.where(place >= first_start, kx_ref[...].astype(jnp.float32), 0.0).astype(
        jnp.bfloat16
    )
    whole()


def far(chip_row, block, ends, qp_ref, kp_ref, vx_ref, source_ref, state_ref):
    keys = kp_ref.shape[0]
    width = qp_ref.shape[1]

    @pl.loop(0, state_ref.shape[0] // (2 * WIDE))
    def _(tile):
        first = tile * 2 * WIDE
        top = chip_row + first
        needed = (top + 2 * WIDE - 1 >= block + REACH) & (block + keys > starts_of(top, ends))

        @pl.when(needed)
        def _():
            tiles = []
            shape = (WIDE, GROUP)
            col = lax.broadcasted_iota(jnp.int32, (WIDE, keys), 1)
            for half in (0, WIDE):
                rows = pl.ds(pl.multiple_of(first + half, WIDE), WIDE)
                query = qp_ref[rows, :]
                conv = dot_t(query, kp_ref[:, 0:width]) + dot_t(query, kp_ref[:, width:])
                row = top + half + lax.broadcasted_iota(jnp.int32, shape, 0)
                start = widen(starts_of(row, ends) - block, keys // GROUP)
                row = widen(row - (REACH + block), keys // GROUP)
                logits = jnp.where((col <= row) & (col >= start), conv, MASKED)
                tiles.append((rows, logits, vx_ref[HALO : HALO + keys, :]))
            absorb(tiles, source_ref, state_ref)

        if source_ref is not state_ref:

            @pl.when(jnp.logical_not(needed))
            def _():
                rows = pl.ds(pl.multiple_of(first, WIDE), 2 * WIDE)
                state_ref[rows, :] = source_ref[rows, :]


def ends_of(place_ref):
    ends = [place_ref[2]]
    for d in range(1, 7):
        ends.append(ends[-1] + place_ref[2 + d])
    return ends


def local_kernel(
    place_ref, taps_ref, own_ref, other_ref, edge_ref, a_ref, b_ref,
    qp_ref, state_ref, done_ref,
    qx_ref, start_ref, kx_ref, vx_ref, kp_ref,
):
    chip_row, block = place_ref[0], place_ref[1]
    core = place_ref[9]
    ends = ends_of(place_ref)
    keys = kp_ref.shape[0]
    taps, key_taps = taps_ref.shape[1:]
    rim = (key_taps - 1) // 2
    done_ref[...] = jnp.zeros(done_ref.shape, jnp.float32)

    @pl.when(core == 0)
    def _():
        qx_ref[0:HALO, :] = edge_ref[HALO:, :].astype(jnp.float32)
        qx_ref[HALO : HALO + keys, :] = own_ref[...].astype(jnp.float32)
        qx_ref[HALO + keys :, :] = other_ref[0:keys, :].astype(jnp.float32)

    @pl.when(core != 0)
    def _():
        qx_ref[0:HALO, :] = other_ref[keys:, :].astype(jnp.float32)
        qx_ref[HALO : HALO + keys, :] = other_ref[0:keys, :].astype(jnp.float32)
        qx_ref[HALO + keys :, :] = own_ref[...].astype(jnp.float32)

    count = state_ref.shape[0]
    for u in range(taps):
        qp_ref[0:count, u * HEAD_DIM : (u + 1) * HEAD_DIM] = qx_ref[
            HALO - u : HALO - u + count, :
        ].astype(jnp.bfloat16)
    lane = lax.broadcasted_iota(jnp.int32, (8, 256), 1)
    for u in range(taps):
        base = jnp.zeros(lane.shape, jnp.float32)
        for t in range(key_taps):
            tap = taps_ref[0, u, t] * SCALE
            if u == 0 and t == rim:
                tap = tap + SCALE
            base = jnp.where(lane == HALO + rim - t, tap, base)
        band = jnp.concatenate([base] * (GROUP // 8), axis=0)
        band = pltpu.roll(band, 0, 1, stride=1, stride_axis=0)
        high = band.astype(jnp.bfloat16)
        qp_ref[taps_at(qp_ref, 0, u)] = high
        qp_ref[taps_at(qp_ref, 1, u)] = (band - high.astype(jnp.float32)).astype(jnp.bfloat16)
    lane = lax.broadcasted_iota(jnp.int32, (count, 128), 1)
    state_ref[:, 0 : 2 * HEAD_DIM] = jnp.zeros((count, 2 * HEAD_DIM), jnp.float32)
    state_ref[:, 2 * HEAD_DIM :] = jnp.where(lane < 64, FLOOR, 0.0)
    lay_keys(a_ref, b_ref, kx_ref, vx_ref)

    @pl.loop(0, keys // BAND + 1)
    def _(tile):
        a = tile * BAND

        @pl.when(block - chip_row + a < count)
        def _():
            near(a, chip_row, block, ends, taps_ref, qp_ref, kx_ref, vx_ref, start_ref, state_ref)

    convolve(True, block, 0, ends, qp_ref, kx_ref, kp_ref)
    far(chip_row, block, ends, qp_ref, kp_ref, vx_ref, state_ref, state_ref)


def hop_kernel(first, last, place_ref, taps_ref, qp_ref, a_ref, b_ref, state_in, *rest):
    if last:
        keep_ref, send_ref, start_ref, kx_ref, vx_ref, kp_ref, state_ref = rest
    else:
        state_ref, done_ref, start_ref, kx_ref, vx_ref, kp_ref = rest
        done_ref[...] = jnp.zeros(done_ref.shape, jnp.float32)
    chip_row, block = place_ref[0], place_ref[1]
    ends = ends_of(place_ref)
    keys = kp_ref.shape[0]
    first_start = starts_of(chip_row, ends)
    active = block + keys > first_start
    if first:
        state_ref[...] = state_in[...]
    else:

        @pl.when(jnp.logical_not(active))
        def _():
            state_ref[...] = state_in[...]

    @pl.when(active)
    def _():
        lay_keys(a_ref, b_ref, kx_ref, vx_ref)
        if first:

            @pl.when(block + keys == chip_row)
            def _():
                near(
                    keys, chip_row, block, ends, taps_ref, qp_ref, kx_ref, vx_ref, start_ref,
                    state_ref,
                )

        convolve(False, block, first_start, ends, qp_ref, kx_ref, kp_ref)
        source = state_ref if first else state_in
        far(chip_row, block, ends, qp_ref, kp_ref, vx_ref, source, state_ref)

    if last:
        core = place_ref[9]
        for ref, side in ((keep_ref, core), (send_ref, 1 - core)):
            ref[...] = state_ref[pl.ds(pl.multiple_of(side * keys, keys), keys), :]


def join_kernel(keep_ref, other_ref, own_ref, cross_ref):
    wide = 2 * HEAD_DIM
    stats, more = keep_ref[:, wide:], other_ref[:, wide:]
    m_a, l_a = stats[:, 0:1], stats[:, 64:65]
    m_b, l_b = more[:, 0:1], more[:, 64:65]
    m = jnp.maximum(m_a, m_b)
    f_a, f_b = jnp.exp(m_a - m), jnp.exp(m_b - m)
    share = 1.0 / (l_a * f_a + l_b * f_b)
    f_a, f_b = f_a * share, f_b * share
    own_ref[...] = keep_ref[:, :HEAD_DIM] * f_a + other_ref[:, :HEAD_DIM] * f_b
    cross_ref[...] = (
        keep_ref[:, HEAD_DIM:wide] * f_a + other_ref[:, HEAD_DIM:wide] * f_b
    ).astype(jnp.bfloat16)


def finish_kernel(mixing_ref, own_ref, cross_ref, gain_ref, out_ref):
    mixed = mixing_ref[0] * own_ref[...] + mixing_ref[1] * cross_ref[...].astype(jnp.float32)
    mean = jnp.mean(mixed * mixed, axis=1, keepdims=True)
    out_ref[...] = (mixed * lax.rsqrt(mean + 1e-05) * gain_ref[...]).astype(jnp.bfloat16)


VMEM = pl.BlockSpec(memory_space=pltpu.VMEM)
SMEM = pl.BlockSpec(memory_space=pltpu.SMEM)


def call(kernel, specs, out, scratch, args, flops=0):
    shapes = [jax.ShapeDtypeStruct(shape, dtype) for shape, dtype in out]
    return pl.pallas_call(
        kernel,
        out_shape=shapes,
        in_specs=specs,
        out_specs=[VMEM] * len(shapes),
        scratch_shapes=scratch,
        cost_estimate=pl.CostEstimate(flops=flops, bytes_accessed=4 << 20, transcendentals=0),
        compiler_params=pltpu.CompilerParams(vmem_limit_bytes=20 << 20),
    )(*args)


def body(queries, key_vectors, values, kernel, mixing, norm_gain, doc_lengths):
    rows = queries.shape[0]
    bf16, f32 = jnp.bfloat16, jnp.float32
    count = lax.axis_size("ctx")
    heads = lax.axis_size("head")
    group = lax.axis_index("ctx")
    core = group % 2
    taps = kernel.shape[1]
    width = taps * HEAD_DIM

    def permute(value, pairs):
        return lax.ppermute(value, "ctx", pairs)

    def onward(value):
        return permute(value, [(i, (i + 2) % count) for i in range(count)])

    def partner(value):
        return lax.ppermute(value, "head", [(i, i ^ (heads // 2)) for i in range(heads)])

    def step(value, by):
        return permute(value, [(i, (i + by) % count) for i in range(count)])

    other_values = partner(values)
    beyond = step(key_vectors[:HALO], -1)
    behind = step(jnp.concatenate([key_vectors[rows - HALO :], queries[rows - HALO :]]), 1)
    sibling = permute(
        jnp.concatenate([queries, behind[HALO:]]), [(i, i ^ 1) for i in range(count)]
    )
    ring_a = jnp.concatenate([key_vectors, behind[:HALO], beyond])
    ring_b = jnp.concatenate([values, other_values])
    chip = group // 2

    def place(hop):
        head = jnp.stack([chip * 2 * rows, (chip - hop) * 2 * rows + core * rows])
        return jnp.concatenate([head, doc_lengths[:7], core[None]]).astype(jnp.int32)

    state = [((2 * rows, 3 * HEAD_DIM), f32)]
    mark = [((8, 128), f32)]
    scratch = [
        pltpu.VMEM((BAND + 8, GROUP), jnp.int32),
        pltpu.VMEM((rows + 128, HEAD_DIM), bf16),
        pltpu.VMEM((rows + 2 * HALO, 2 * HEAD_DIM), bf16),
        pltpu.VMEM((rows, 2 * width), bf16),
    ]
    flops = 2 * 2 * rows * rows * (2 * width + 2 * HEAD_DIM)
    operand, running, done = call(
        local_kernel,
        [SMEM, SMEM] + [VMEM] * 5,
        [((2 * rows + 2 * taps * GROUP * 256 // width, width), bf16)]
        + state
        + mark,
        [pltpu.VMEM((2 * rows + HALO, HEAD_DIM), f32)] + scratch,
        (place(0), kernel, queries, sibling, behind, ring_a, ring_b),
        flops=flops,
    )
    for hop in range(1, HOPS + 1):
        ring_a, ring_b = onward(ring_a), onward(ring_b)
        ring_a, _ = lax.optimization_barrier((ring_a, done))
        ring_b, _ = lax.optimization_barrier((ring_b, done))
        last = hop == HOPS
        out = [((rows, 3 * HEAD_DIM), f32)] * 2 if last else state + mark
        extra = [pltpu.VMEM(shape, dtype) for shape, dtype in state] if last else []
        result = call(
            functools.partial(hop_kernel, hop == 1, last),
            [SMEM, SMEM] + [VMEM] * 4,
            out,
            scratch + extra,
            (place(hop), kernel, operand, ring_a, ring_b, running),
            flops=flops,
        )
        if not last:
            running, done = result
    keep, send = result
    other = permute(send, [(i, i ^ 1) for i in range(count)])
    own, cross = call(
        join_kernel,
        [VMEM, VMEM],
        [((rows, HEAD_DIM), f32), ((rows, HEAD_DIM), bf16)],
        [],
        (keep, other),
    )
    (finished,) = call(
        finish_kernel,
        [SMEM, VMEM, VMEM, VMEM],
        [((rows, HEAD_DIM), bf16)],
        [],
        (mixing.reshape(-1), own, partner(cross), norm_gain.reshape(1, HEAD_DIM)),
    )
    return finished


def solution(mesh):
    return jax.shard_map(
        body,
        mesh=mesh,
        in_specs=(
            P("ctx", "head"),
            P("ctx", "head"),
            P("ctx", "head"),
            P("head", None, None),
            P("head", None),
            P("head"),
            P(),
        ),
        out_specs=P("ctx", "head"),
        check_vma=False,
    )
```

```python
import functools

import jax
import jax.numpy as jnp
from jax import lax
from jax.experimental import pallas as pl
from jax.experimental.pallas import tpu as pltpu
from jax.sharding import PartitionSpec as P

HEAD_DIM = 128
SCALE = HEAD_DIM ** (-0.5)
MASKED = -1e30
FLOOR = -1e20
HALO = 16
BAND = 64
TILES = 4
GROUP = 128
WIDE = 256
REACH = 10
HOPS = 4


def dot(a, b):
    return lax.dot_general(a, b, (((1,), (0,)), ((), ())), preferred_element_type=jnp.float32)


def dot_t(a, b):
    return lax.dot_general(a, b, (((1,), (1,)), ((), ())), preferred_element_type=jnp.float32)


def starts_of(position, ends):
    start = jnp.zeros_like(position)
    for end in ends:
        start = jnp.where(position >= end, end, start)
    return start


def widen(column, times):
    return jnp.concatenate([column] * times, axis=1) if times > 1 else column


def absorb(tiles, source_ref, state_ref):
    wide = 2 * HEAD_DIM
    done = []
    for rows, logits, values in tiles:
        m_old = source_ref[rows, wide : wide + 1]
        m_new = jnp.maximum(m_old, jnp.max(logits, axis=1, keepdims=True))
        weights = jnp.exp(logits - m_new)
        factor = jnp.exp(m_old - m_new)
        total = source_ref[rows, wide + 64 : wide + 65] * factor
        total = total + jnp.sum(weights, axis=1, keepdims=True)
        product = dot(weights.astype(jnp.bfloat16), values)
        product = source_ref[rows, 0:wide] * factor + product
        lane = lax.broadcasted_iota(jnp.int32, (logits.shape[0], 128), 1)
        done.append((rows, jnp.where(lane < 64, m_new, total), product))
    for rows, stats, product in done:
        state_ref[rows, 0:wide] = product
        state_ref[rows, wide:] = stats


def taps_at(qp_ref, rest, u):
    most = qp_ref.shape[1] // 256
    sets = qp_ref.shape[1] // HEAD_DIM // most
    row = qp_ref.shape[0] - (2 - rest) * sets * GROUP + u // most * GROUP
    return slice(row, row + GROUP), slice(u % most * 256, u % most * 256 + 256)


def lay_keys(a_ref, b_ref, kx_ref, vx_ref):
    keys = a_ref.shape[0]
    kx_ref[0:HALO, :] = b_ref[2 * keys : 2 * keys + HALO, :]
    kx_ref[HALO : HALO + keys, :] = a_ref[...]
    kx_ref[HALO + keys : 2 * HALO + keys, :] = b_ref[2 * keys + HALO :, :]
    kx_ref[2 * HALO + keys :, :] = jnp.zeros_like(kx_ref[2 * HALO + keys :, :])
    vx_ref[0:HALO, :] = jnp.zeros((HALO, 2 * HEAD_DIM), jnp.bfloat16)
    vx_ref[HALO : HALO + keys, 0:HEAD_DIM] = b_ref[0:keys, :]
    vx_ref[HALO : HALO + keys, HEAD_DIM:] = b_ref[keys : 2 * keys, :]
    vx_ref[HALO + keys :, :] = jnp.zeros_like(vx_ref[HALO + keys :, :])


def near(tiles, chip_row, block, ends, taps_ref, qp_ref, kx_ref, vx_ref, start_ref, state_ref):
    keys = kx_ref.shape[0] - 128
    query_taps, key_taps = taps_ref.shape[1:]
    rim = (key_taps - 1) // 2
    half = BAND // 2
    shape = (half, GROUP)
    for n, a in enumerate(tiles):
        top = block + a
        one_start = starts_of(top + BAND - 1, ends)
        one = starts_of(top - 8, ends) == one_start

        @pl.when(one)
        def _(n=n, one_start=one_start):
            start_ref[n] = jnp.full(start_ref.shape[1:], one_start, jnp.int32)

        @pl.when(jnp.logical_not(one))
        def _(n=n, top=top):
            side = lax.broadcasted_iota(jnp.int32, start_ref.shape[1:], 1) >= 64
            position = top - 8 + lax.broadcasted_iota(jnp.int32, start_ref.shape[1:], 0)
            start_ref[n] = starts_of(position + jnp.where(side, half, 0), ends)

    lane = lax.broadcasted_iota(jnp.int32, shape, 1)
    left = lane < 64
    shift = jnp.where(left, 0, half)
    step = lax.broadcasted_iota(jnp.int32, shape, 0) + shift
    place = lane - HALO - shift
    behind = step - place
    work = []
    for n, a in enumerate(tiles):
        rows = pl.ds(pl.multiple_of(block - chip_row + a, 16), BAND)
        parts = [
            (pl.ds(pl.multiple_of(a + m, 16), 64), pl.ds(pl.multiple_of(block - chip_row + a + m, 16), half))
            for m in (0, half)
        ]
        stacked = jnp.concatenate(
            [
                qp_ref[part, u * HEAD_DIM : (u + 1) * HEAD_DIM]
                for _, part in parts
                for u in range(query_taps)
            ],
            axis=0,
        )
        window = jnp.concatenate([kx_ref[span, :] for span, _ in parts], axis=0)
        values = jnp.concatenate([vx_ref[span, :] for span, _ in parts], axis=0)
        work.append((n, rows, block + a + place, dot_t(stacked, window), values))
    done = []
    for n, rows, col, products, values in work:
        scores = []
        for u in range(query_taps):
            both = [products[(m * query_taps + u) * half :][:half] for m in (0, 1)]
            allowed = (behind >= u) & (col >= start_ref[n, 8 - u : 8 - u + half, :])
            scores.append(jnp.where(allowed, jnp.where(left, *both), 0.0))
        conv = None
        for t in range(key_taps):
            terms = None
            for u in range(query_taps):
                tap = taps_ref[0, u, t] * SCALE
                if u == 0 and t == rim:
                    tap = tap + SCALE
                terms = scores[u] * tap if terms is None else terms + scores[u] * tap
            if t != rim:
                terms = pltpu.roll(terms, (t - rim) % GROUP, 1)
            conv = terms if conv is None else conv + terms
        inside = (col >= block) & (col < block + keys) & (col >= start_ref[n, 8 : 8 + half, :])
        inside = inside & (behind >= 0) & (behind < REACH)
        logits = jnp.concatenate(
            [
                jnp.where(inside & left, conv, MASKED),
                jnp.where(inside & jnp.logical_not(left), conv, MASKED),
            ],
            axis=0,
        )
        done.append((rows, logits, values))
    absorb(done, state_ref, state_ref)


def convolve(local, block, first_start, ends, qp_ref, kx_ref, kp_ref):
    total = kx_ref.shape[0]
    keys = kp_ref.shape[0]
    width = kp_ref.shape[1] // 2
    taps = width // HEAD_DIM
    depth = 256
    def put(g, u, done):
        top = done.astype(jnp.bfloat16)
        rest = (done - top.astype(jnp.float32)).astype(jnp.bfloat16)
        for n in range(done.shape[1] // HEAD_DIM):
            here = slice((g + n) * GROUP, (g + n + 1) * GROUP)
            lanes = slice(n * HEAD_DIM, (n + 1) * HEAD_DIM)
            kp_ref[here, u * HEAD_DIM : (u + 1) * HEAD_DIM] = top[:, lanes]
            kp_ref[here, width + u * HEAD_DIM : width + (u + 1) * HEAD_DIM] = rest[:, lanes]

    def whole():
        for g in range(0, keys // GROUP, 2):
            window = jnp.concatenate(
                [kx_ref[n * GROUP : n * GROUP + depth, :] for n in (g, g + 1)], axis=1
            )
            for u in range(taps):
                high, rest = (qp_ref[taps_at(qp_ref, n, u)] for n in (0, 1))
                put(g, u, dot(high, window) + dot(rest, window))

    def cut():
        for g in range(keys // GROUP):
            shape = (GROUP, depth)
            out = block + g * GROUP + lax.broadcasted_iota(jnp.int32, shape, 0)
            inp = block + g * GROUP - HALO + lax.broadcasted_iota(jnp.int32, shape, 1)
            keep = inp >= starts_of(out, ends)
            window = kx_ref[g * GROUP : g * GROUP + depth, :]
            for u in range(taps):
                high, rest = (
                    jnp.where(keep, qp_ref[taps_at(qp_ref, n, u)].astype(jnp.float32), 0.0).astype(
                        jnp.bfloat16
                    )
                    for n in (0, 1)
                )
                put(g, u, dot(high, window) + dot(rest, window))

    if local:
        unbroken = starts_of(block + keys - 1, ends) <= block - HALO

        @pl.when(unbroken)
        def _():
            whole()

        @pl.when(jnp.logical_not(unbroken))
        def _():
            cut()

        return
    place = block - HALO + lax.broadcasted_iota(jnp.int32, (total, HEAD_DIM), 0)
    kx_ref[...] = jnp.where(place >= first_start, kx_ref[...].astype(jnp.float32), 0.0).astype(
        jnp.bfloat16
    )
    whole()


def far(chip_row, block, ends, qp_ref, kp_ref, vx_ref, source_ref, state_ref):
    keys = kp_ref.shape[0]
    width = qp_ref.shape[1]

    @pl.loop(0, state_ref.shape[0] // (2 * WIDE))
    def _(tile):
        first = tile * 2 * WIDE
        top = chip_row + first
        needed = (top + 2 * WIDE - 1 >= block + REACH) & (block + keys > starts_of(top, ends))

        @pl.when(needed)
        def _():
            tiles = []
            shape = (WIDE, GROUP)
            col = lax.broadcasted_iota(jnp.int32, (WIDE, keys), 1)
            for half in (0, WIDE):
                rows = pl.ds(pl.multiple_of(first + half, WIDE), WIDE)
                query = qp_ref[rows, :]
                conv = dot_t(query, kp_ref[:, 0:width]) + dot_t(query, kp_ref[:, width:])
                row = top + half + lax.broadcasted_iota(jnp.int32, shape, 0)
                start = widen(starts_of(row, ends) - block, keys // GROUP)
                row = widen(row - (REACH + block), keys // GROUP)
                logits = jnp.where((col <= row) & (col >= start), conv, MASKED)
                tiles.append((rows, logits, vx_ref[HALO : HALO + keys, :]))
            absorb(tiles, source_ref, state_ref)

        if source_ref is not state_ref:

            @pl.when(jnp.logical_not(needed))
            def _():
                rows = pl.ds(pl.multiple_of(first, WIDE), 2 * WIDE)
                state_ref[rows, :] = source_ref[rows, :]


def ends_of(place_ref):
    ends = [place_ref[2]]
    for d in range(1, 7):
        ends.append(ends[-1] + place_ref[2 + d])
    return ends


def local_kernel(
    place_ref, taps_ref, own_ref, other_ref, edge_ref, a_ref, b_ref,
    qp_ref, state_ref, done_ref,
    qx_ref, start_ref, kx_ref, vx_ref, kp_ref,
):
    chip_row, block = place_ref[0], place_ref[1]
    core = place_ref[9]
    ends = ends_of(place_ref)
    keys = kp_ref.shape[0]
    taps, key_taps = taps_ref.shape[1:]
    rim = (key_taps - 1) // 2
    done_ref[...] = jnp.zeros(done_ref.shape, jnp.float32)

    @pl.when(core == 0)
    def _():
        qx_ref[0:HALO, :] = edge_ref[HALO:, :].astype(jnp.float32)
        qx_ref[HALO : HALO + keys, :] = own_ref[...].astype(jnp.float32)
        qx_ref[HALO + keys :, :] = other_ref[0:keys, :].astype(jnp.float32)

    @pl.when(core != 0)
    def _():
        qx_ref[0:HALO, :] = other_ref[keys:, :].astype(jnp.float32)
        qx_ref[HALO : HALO + keys, :] = other_ref[0:keys, :].astype(jnp.float32)
        qx_ref[HALO + keys :, :] = own_ref[...].astype(jnp.float32)

    count = state_ref.shape[0]
    for u in range(taps):
        qp_ref[0:count, u * HEAD_DIM : (u + 1) * HEAD_DIM] = qx_ref[
            HALO - u : HALO - u + count, :
        ].astype(jnp.bfloat16)
    lane = lax.broadcasted_iota(jnp.int32, (8, 256), 1)
    for u in range(taps):
        base = jnp.zeros(lane.shape, jnp.float32)
        for t in range(key_taps):
            tap = taps_ref[0, u, t] * SCALE
            if u == 0 and t == rim:
                tap = tap + SCALE
            base = jnp.where(lane == HALO + rim - t, tap, base)
        band = jnp.concatenate([base] * (GROUP // 8), axis=0)
        band = pltpu.roll(band, 0, 1, stride=1, stride_axis=0)
        high = band.astype(jnp.bfloat16)
        qp_ref[taps_at(qp_ref, 0, u)] = high
        qp_ref[taps_at(qp_ref, 1, u)] = (band - high.astype(jnp.float32)).astype(jnp.bfloat16)
    lane = lax.broadcasted_iota(jnp.int32, (count, 128), 1)
    state_ref[:, 0 : 2 * HEAD_DIM] = jnp.zeros((count, 2 * HEAD_DIM), jnp.float32)
    state_ref[:, 2 * HEAD_DIM :] = jnp.where(lane < 64, FLOOR, 0.0)
    lay_keys(a_ref, b_ref, kx_ref, vx_ref)

    rest = (chip_row, block, ends, taps_ref, qp_ref, kx_ref, vx_ref, start_ref, state_ref)

    @pl.loop(0, keys // (BAND * TILES))
    def _(step):
        near([(step * TILES + n) * BAND for n in range(TILES)], *rest)

    @pl.when(block + keys - chip_row < count)
    def _():
        near([keys], *rest)

    convolve(True, block, 0, ends, qp_ref, kx_ref, kp_ref)
    far(chip_row, block, ends, qp_ref, kp_ref, vx_ref, state_ref, state_ref)


def hop_kernel(first, last, place_ref, taps_ref, qp_ref, a_ref, b_ref, state_in, *rest):
    if last:
        keep_ref, send_ref, start_ref, kx_ref, vx_ref, kp_ref, state_ref = rest
    else:
        state_ref, done_ref, start_ref, kx_ref, vx_ref, kp_ref = rest
        done_ref[...] = jnp.zeros(done_ref.shape, jnp.float32)
    chip_row, block = place_ref[0], place_ref[1]
    ends = ends_of(place_ref)
    keys = kp_ref.shape[0]
    first_start = starts_of(chip_row, ends)
    active = block + keys > first_start
    if first:
        state_ref[...] = state_in[...]
    else:

        @pl.when(jnp.logical_not(active))
        def _():
            state_ref[...] = state_in[...]

    @pl.when(active)
    def _():
        lay_keys(a_ref, b_ref, kx_ref, vx_ref)
        if first:

            @pl.when(block + keys == chip_row)
            def _():
                near(
                    [keys], chip_row, block, ends, taps_ref, qp_ref, kx_ref, vx_ref, start_ref,
                    state_ref,
                )

        convolve(False, block, first_start, ends, qp_ref, kx_ref, kp_ref)
        source = state_ref if first else state_in
        far(chip_row, block, ends, qp_ref, kp_ref, vx_ref, source, state_ref)

    if last:
        core = place_ref[9]
        for ref, side in ((keep_ref, core), (send_ref, 1 - core)):
            ref[...] = state_ref[pl.ds(pl.multiple_of(side * keys, keys), keys), :]


def join_kernel(keep_ref, other_ref, own_ref, cross_ref):
    wide = 2 * HEAD_DIM
    stats, more = keep_ref[:, wide:], other_ref[:, wide:]
    m_a, l_a = stats[:, 0:1], stats[:, 64:65]
    m_b, l_b = more[:, 0:1], more[:, 64:65]
    m = jnp.maximum(m_a, m_b)
    f_a, f_b = jnp.exp(m_a - m), jnp.exp(m_b - m)
    share = 1.0 / (l_a * f_a + l_b * f_b)
    f_a, f_b = f_a * share, f_b * share
    own_ref[...] = keep_ref[:, :HEAD_DIM] * f_a + other_ref[:, :HEAD_DIM] * f_b
    cross_ref[...] = (
        keep_ref[:, HEAD_DIM:wide] * f_a + other_ref[:, HEAD_DIM:wide] * f_b
    ).astype(jnp.bfloat16)


def finish_kernel(mixing_ref, own_ref, cross_ref, gain_ref, out_ref):
    mixed = mixing_ref[0] * own_ref[...] + mixing_ref[1] * cross_ref[...].astype(jnp.float32)
    mean = jnp.mean(mixed * mixed, axis=1, keepdims=True)
    out_ref[...] = (mixed * lax.rsqrt(mean + 1e-05) * gain_ref[...]).astype(jnp.bfloat16)


VMEM = pl.BlockSpec(memory_space=pltpu.VMEM)
SMEM = pl.BlockSpec(memory_space=pltpu.SMEM)


def call(kernel, specs, out, scratch, args, flops=0):
    shapes = [jax.ShapeDtypeStruct(shape, dtype) for shape, dtype in out]
    return pl.pallas_call(
        kernel,
        out_shape=shapes,
        in_specs=specs,
        out_specs=[VMEM] * len(shapes),
        scratch_shapes=scratch,
        cost_estimate=pl.CostEstimate(flops=8 * flops, bytes_accessed=4 << 20, transcendentals=0),
        compiler_params=pltpu.CompilerParams(vmem_limit_bytes=20 << 20),
    )(*args)


def body(queries, key_vectors, values, kernel, mixing, norm_gain, doc_lengths):
    rows = queries.shape[0]
    bf16, f32 = jnp.bfloat16, jnp.float32
    count = lax.axis_size("ctx")
    heads = lax.axis_size("head")
    group = lax.axis_index("ctx")
    core = group % 2
    taps = kernel.shape[1]
    width = taps * HEAD_DIM

    def permute(value, pairs):
        return lax.ppermute(value, "ctx", pairs)

    def onward(value):
        return permute(value, [(i, (i + 2) % count) for i in range(count)])

    def partner(value):
        return lax.ppermute(value, "head", [(i, i ^ (heads // 2)) for i in range(heads)])

    def step(value, by):
        return permute(value, [(i, (i + by) % count) for i in range(count)])

    other_values = partner(values)
    beyond = step(key_vectors[:HALO], -1)
    behind = step(jnp.concatenate([key_vectors[rows - HALO :], queries[rows - HALO :]]), 1)
    sibling = permute(
        jnp.concatenate([queries, behind[HALO:]]), [(i, i ^ 1) for i in range(count)]
    )
    ring_a = key_vectors
    ring_b = jnp.concatenate([values, other_values, behind[:HALO], beyond])
    chip = group // 2

    def place(hop):
        head = jnp.stack([chip * 2 * rows, (chip - hop) * 2 * rows + core * rows])
        return jnp.concatenate([head, doc_lengths[:7], core[None]]).astype(jnp.int32)

    state = [((2 * rows, 3 * HEAD_DIM), f32)]
    mark = [((8, 128), f32)]
    scratch = [
        pltpu.VMEM((TILES, BAND // 2 + 8, GROUP), jnp.int32),
        pltpu.VMEM((rows + 128, HEAD_DIM), bf16),
        pltpu.VMEM((rows + 128, 2 * HEAD_DIM), bf16),
        pltpu.VMEM((rows, 2 * width), bf16),
    ]
    flops = 2 * 2 * rows * rows * (2 * width + 2 * HEAD_DIM)
    operand, running, done = call(
        local_kernel,
        [SMEM, SMEM] + [VMEM] * 5,
        [((2 * rows + 2 * taps * GROUP * 256 // width, width), bf16)]
        + state
        + mark,
        [pltpu.VMEM((2 * rows + HALO, HEAD_DIM), f32)] + scratch,
        (place(0), kernel, queries, sibling, behind, ring_a, ring_b),
        flops=8 * flops,
    )
    for hop in range(1, HOPS + 1):
        ring_a, ring_b = onward(ring_a), onward(ring_b)
        ring_a, _ = lax.optimization_barrier((ring_a, done))
        ring_b, _ = lax.optimization_barrier((ring_b, done))
        last = hop == HOPS
        out = [((rows, 3 * HEAD_DIM), f32)] * 2 if last else state + mark
        extra = [pltpu.VMEM(shape, dtype) for shape, dtype in state] if last else []
        result = call(
            functools.partial(hop_kernel, hop == 1, last),
            [SMEM, SMEM] + [VMEM] * 4,
            out,
            scratch + extra,
            (place(hop), kernel, operand, ring_a, ring_b, running),
            flops=8 * flops,
        )
        if not last:
            running, done = result
    keep, send = result
    other = permute(send, [(i, i ^ 1) for i in range(count)])
    own, cross = call(
        join_kernel,
        [VMEM, VMEM],
        [((rows, HEAD_DIM), f32), ((rows, HEAD_DIM), bf16)],
        [],
        (keep, other),
    )
    (finished,) = call(
        finish_kernel,
        [SMEM, VMEM, VMEM, VMEM],
        [((rows, HEAD_DIM), bf16)],
        [],
        (mixing.reshape(-1), own, partner(cross), norm_gain.reshape(1, HEAD_DIM)),
    )
    return finished


def solution(mesh):
    return jax.shard_map(
        body,
        mesh=mesh,
        in_specs=(
            P("ctx", "head"),
            P("ctx", "head"),
            P("ctx", "head"),
            P("head", None, None),
            P("head", None),
            P("head"),
            P(),
        ),
        out_specs=P("ctx", "head"),
        check_vma=False,
    )
```

```python
import functools

import jax
import jax.numpy as jnp
from jax import lax
from jax.experimental import pallas as pl
from jax.experimental.pallas import tpu as pltpu
from jax.sharding import PartitionSpec as P

HEAD_DIM = 128
SCALE = HEAD_DIM ** (-0.5)
MASKED = -1e30
FLOOR = -1e20
HALO = 16
BAND = 64
TILES = 4
GROUP = 128
WIDE = 256
REACH = 10
HOPS = 4


def dot(a, b):
    return lax.dot_general(a, b, (((1,), (0,)), ((), ())), preferred_element_type=jnp.float32)


def dot_t(a, b):
    return lax.dot_general(a, b, (((1,), (1,)), ((), ())), preferred_element_type=jnp.float32)


def starts_of(position, ends):
    start = jnp.zeros_like(position)
    for end in ends:
        start = jnp.where(position >= end, end, start)
    return start


def widen(column, times):
    return jnp.concatenate([column] * times, axis=1) if times > 1 else column


def absorb(tiles, source_ref, state_ref):
    wide = 2 * HEAD_DIM
    done = []
    for rows, logits, values in tiles:
        m_old = source_ref[rows, wide : wide + 1]
        m_new = jnp.maximum(m_old, jnp.max(logits, axis=1, keepdims=True))
        weights = jnp.exp(logits - m_new)
        factor = jnp.exp(m_old - m_new)
        total = source_ref[rows, wide + 64 : wide + 65] * factor
        total = total + jnp.sum(weights, axis=1, keepdims=True)
        product = dot(weights.astype(jnp.bfloat16), values)
        product = source_ref[rows, 0:wide] * factor + product
        lane = lax.broadcasted_iota(jnp.int32, (logits.shape[0], 128), 1)
        done.append((rows, jnp.where(lane < 64, m_new, total), product))
    for rows, stats, product in done:
        state_ref[rows, 0:wide] = product
        state_ref[rows, wide:] = stats


def taps_at(qp_ref, rest, u):
    most = qp_ref.shape[1] // 256
    sets = qp_ref.shape[1] // HEAD_DIM // most
    row = qp_ref.shape[0] - (2 - rest) * sets * GROUP + u // most * GROUP
    return slice(row, row + GROUP), slice(u % most * 256, u % most * 256 + 256)


def lay_keys(a_ref, b_ref, kx_ref, vx_ref):
    keys = kx_ref.shape[0] - 128
    kx_ref[0:HALO, :] = b_ref[2 * keys : 2 * keys + HALO, :]
    if a_ref is not None:
        kx_ref[HALO : HALO + keys, :] = a_ref[...]
    kx_ref[HALO + keys : 2 * HALO + keys, :] = b_ref[2 * keys + HALO :, :]
    kx_ref[2 * HALO + keys :, :] = jnp.zeros_like(kx_ref[2 * HALO + keys :, :])
    vx_ref[0:HALO, :] = jnp.zeros((HALO, 2 * HEAD_DIM), jnp.bfloat16)
    vx_ref[HALO : HALO + keys, 0:HEAD_DIM] = b_ref[0:keys, :]
    vx_ref[HALO : HALO + keys, HEAD_DIM:] = b_ref[keys : 2 * keys, :]
    vx_ref[HALO + keys :, :] = jnp.zeros_like(vx_ref[HALO + keys :, :])


def near(tiles, chip_row, block, ends, taps_ref, qp_ref, kx_ref, vx_ref, start_ref, state_ref):
    keys = kx_ref.shape[0] - 128
    query_taps, _, key_taps = taps_ref.shape
    rim = (key_taps - 1) // 2
    half = BAND // 2
    shape = (half, GROUP)
    for n, a in enumerate(tiles):
        top = block + a
        one_start = starts_of(top + BAND - 1, ends)
        one = starts_of(top - 8, ends) == one_start

        @pl.when(one)
        def _(n=n, one_start=one_start):
            start_ref[n] = jnp.full(start_ref.shape[1:], one_start, jnp.int32)

        @pl.when(jnp.logical_not(one))
        def _(n=n, top=top):
            side = lax.broadcasted_iota(jnp.int32, start_ref.shape[1:], 1) >= 64
            position = top - 8 + lax.broadcasted_iota(jnp.int32, start_ref.shape[1:], 0)
            start_ref[n] = starts_of(position + jnp.where(side, half, 0), ends)

    lane = lax.broadcasted_iota(jnp.int32, shape, 1)
    left = lane < 64
    shift = jnp.where(left, 0, half)
    step = lax.broadcasted_iota(jnp.int32, shape, 0) + shift
    place = lane - HALO - shift
    behind = step - place
    work = []
    for n, a in enumerate(tiles):
        rows = pl.ds(pl.multiple_of(block - chip_row + a, 16), BAND)
        parts = [
            (pl.ds(pl.multiple_of(a + m, 16), 64), pl.ds(pl.multiple_of(block - chip_row + a + m, 16), half))
            for m in (0, half)
        ]
        stacked = jnp.concatenate(
            [
                qp_ref[part, u * HEAD_DIM : (u + 1) * HEAD_DIM]
                for _, part in parts
                for u in range(query_taps)
            ],
            axis=0,
        )
        window = jnp.concatenate([kx_ref[span, :] for span, _ in parts], axis=0)
        values = jnp.concatenate([vx_ref[span, :] for span, _ in parts], axis=0)
        work.append((n, rows, block + a + place, dot_t(stacked, window), values))
    done = []
    for n, rows, col, products, values in work:
        scores = []
        for u in range(query_taps):
            both = [products[(m * query_taps + u) * half :][:half] for m in (0, 1)]
            allowed = (behind >= u) & (col >= start_ref[n, 8 - u : 8 - u + half, :])
            scores.append(jnp.where(allowed, jnp.where(left, *both), 0.0))
        conv = None
        for t in range(key_taps):
            terms = None
            for u in range(query_taps):
                tap = taps_ref[u, 0, t] * SCALE
                if u == 0 and t == rim:
                    tap = tap + SCALE
                terms = scores[u] * tap if terms is None else terms + scores[u] * tap
            if t != rim:
                terms = pltpu.roll(terms, (t - rim) % GROUP, 1)
            conv = terms if conv is None else conv + terms
        inside = (col >= block) & (col < block + keys) & (col >= start_ref[n, 8 : 8 + half, :])
        inside = inside & (behind >= 0) & (behind < REACH)
        logits = jnp.concatenate(
            [
                jnp.where(inside & left, conv, MASKED),
                jnp.where(inside & jnp.logical_not(left), conv, MASKED),
            ],
            axis=0,
        )
        done.append((rows, logits, values))
    absorb(done, state_ref, state_ref)


def convolve(local, block, first_start, ends, qp_ref, kx_ref, kp_ref):
    total = kx_ref.shape[0]
    keys = kp_ref.shape[0]
    width = kp_ref.shape[1] // 2
    taps = width // HEAD_DIM
    depth = 256
    def put(g, u, done):
        top = done.astype(jnp.bfloat16)
        rest = (done - top.astype(jnp.float32)).astype(jnp.bfloat16)
        for n in range(done.shape[1] // HEAD_DIM):
            here = slice((g + n) * GROUP, (g + n + 1) * GROUP)
            lanes = slice(n * HEAD_DIM, (n + 1) * HEAD_DIM)
            kp_ref[here, u * HEAD_DIM : (u + 1) * HEAD_DIM] = top[:, lanes]
            kp_ref[here, width + u * HEAD_DIM : width + (u + 1) * HEAD_DIM] = rest[:, lanes]

    def whole():
        for g in range(0, keys // GROUP, 2):
            window = jnp.concatenate(
                [kx_ref[n * GROUP : n * GROUP + depth, :] for n in (g, g + 1)], axis=1
            )
            for u in range(taps):
                high, rest = (qp_ref[taps_at(qp_ref, n, u)] for n in (0, 1))
                put(g, u, dot(high, window) + dot(rest, window))

    def cut():
        for g in range(keys // GROUP):
            shape = (GROUP, depth)
            out = block + g * GROUP + lax.broadcasted_iota(jnp.int32, shape, 0)
            inp = block + g * GROUP - HALO + lax.broadcasted_iota(jnp.int32, shape, 1)
            keep = inp >= starts_of(out, ends)
            window = kx_ref[g * GROUP : g * GROUP + depth, :]
            for u in range(taps):
                high, rest = (
                    jnp.where(keep, qp_ref[taps_at(qp_ref, n, u)].astype(jnp.float32), 0.0).astype(
                        jnp.bfloat16
                    )
                    for n in (0, 1)
                )
                put(g, u, dot(high, window) + dot(rest, window))

    if local:
        unbroken = starts_of(block + keys - 1, ends) <= block - HALO

        @pl.when(unbroken)
        def _():
            whole()

        @pl.when(jnp.logical_not(unbroken))
        def _():
            cut()

        return
    place = block - HALO + lax.broadcasted_iota(jnp.int32, (total, HEAD_DIM), 0)
    kx_ref[...] = jnp.where(place >= first_start, kx_ref[...].astype(jnp.float32), 0.0).astype(
        jnp.bfloat16
    )
    whole()


def far(tiles_at_once, chip_row, block, ends, qp_ref, kp_ref, vx_ref, source_ref, state_ref):
    keys = kp_ref.shape[0]
    width = qp_ref.shape[1]
    span = tiles_at_once * WIDE

    @pl.loop(0, state_ref.shape[0] // span)
    def _(tile):
        first = tile * span
        top = chip_row + first
        needed = (top + span - 1 >= block + REACH) & (block + keys > starts_of(top, ends))

        @pl.when(needed)
        def _():
            tiles = []
            shape = (WIDE, GROUP)
            col = lax.broadcasted_iota(jnp.int32, (WIDE, keys), 1)
            for half in range(0, span, WIDE):
                rows = pl.ds(pl.multiple_of(first + half, WIDE), WIDE)
                query = qp_ref[rows, :]
                conv = dot_t(query, kp_ref[:, 0:width]) + dot_t(query, kp_ref[:, width:])
                row = top + half + lax.broadcasted_iota(jnp.int32, shape, 0)
                start = widen(starts_of(row, ends) - block, keys // GROUP)
                row = widen(row - (REACH + block), keys // GROUP)
                logits = jnp.where((col <= row) & (col >= start), conv, MASKED)
                tiles.append((rows, logits, vx_ref[HALO : HALO + keys, :]))
            absorb(tiles, source_ref, state_ref)

        if source_ref is not state_ref:

            @pl.when(jnp.logical_not(needed))
            def _():
                rows = pl.ds(pl.multiple_of(first, WIDE), span)
                state_ref[rows, :] = source_ref[rows, :]


def place_of(hop, rows, docs_ref):
    group = lax.axis_index("ctx")
    core = group & 1
    chip = group >> 1
    ends = [docs_ref[0]]
    for d in range(1, 7):
        ends.append(ends[-1] + docs_ref[d])
    return chip * 2 * rows, core, (chip - hop) * 2 * rows + core * rows, ends


def local_kernel(
    docs_ref, taps_ref, own_ref, other_ref, edge_ref, a_ref, b_ref,
    qp_ref, state_ref, done_ref,
    qx_ref, copied, start_ref, kx_ref, vx_ref, kp_ref,
):
    keys = kp_ref.shape[0]
    chip_row, core, block, ends = place_of(0, keys, docs_ref)
    taken = pltpu.make_async_copy(a_ref, kx_ref.at[pl.ds(HALO, keys), :], copied)
    taken.start()
    taps, _, key_taps = taps_ref.shape
    rim = (key_taps - 1) // 2
    done_ref[...] = jnp.zeros(done_ref.shape, jnp.float32)

    @pl.when(core == 0)
    def _():
        qx_ref[0:HALO, :] = edge_ref[HALO:, :].astype(jnp.float32)
        qx_ref[HALO : HALO + keys, :] = own_ref[0:keys, :].astype(jnp.float32)
        qx_ref[HALO + keys :, :] = other_ref[0:keys, :].astype(jnp.float32)

    @pl.when(core != 0)
    def _():
        qx_ref[0:HALO, :] = other_ref[keys:, :].astype(jnp.float32)
        qx_ref[HALO : HALO + keys, :] = other_ref[0:keys, :].astype(jnp.float32)
        qx_ref[HALO + keys :, :] = own_ref[0:keys, :].astype(jnp.float32)

    count = state_ref.shape[0]
    for u in range(taps):
        qp_ref[0:count, u * HEAD_DIM : (u + 1) * HEAD_DIM] = qx_ref[
            HALO - u : HALO - u + count, :
        ].astype(jnp.bfloat16)
    lane = lax.broadcasted_iota(jnp.int32, (8, 256), 1)
    for u in range(taps):
        base = jnp.zeros(lane.shape, jnp.float32)
        for t in range(key_taps):
            tap = taps_ref[u, 0, t] * SCALE
            if u == 0 and t == rim:
                tap = tap + SCALE
            base = jnp.where(lane == HALO + rim - t, tap, base)
        band = jnp.concatenate([base] * (GROUP // 8), axis=0)
        band = pltpu.roll(band, 0, 1, stride=1, stride_axis=0)
        high = band.astype(jnp.bfloat16)
        qp_ref[taps_at(qp_ref, 0, u)] = high
        qp_ref[taps_at(qp_ref, 1, u)] = (band - high.astype(jnp.float32)).astype(jnp.bfloat16)
    lane = lax.broadcasted_iota(jnp.int32, (count, 128), 1)
    state_ref[:, 0 : 2 * HEAD_DIM] = jnp.zeros((count, 2 * HEAD_DIM), jnp.float32)
    state_ref[:, 2 * HEAD_DIM :] = jnp.where(lane < 64, FLOOR, 0.0)
    lay_keys(None, b_ref, kx_ref, vx_ref)
    taken.wait()
    rest = (chip_row, block, ends, taps_ref, qp_ref, kx_ref, vx_ref, start_ref, state_ref)

    @pl.loop(0, keys // (BAND * TILES))
    def _(step):
        near([(step * TILES + n) * BAND for n in range(TILES)], *rest)

    @pl.when(block + keys - chip_row < count)
    def _():
        near([keys], *rest)

    convolve(True, block, 0, ends, qp_ref, kx_ref, kp_ref)
    far(2, chip_row, block, ends, qp_ref, kp_ref, vx_ref, state_ref, state_ref)


def hop_kernel(hop, last, docs_ref, taps_ref, qp_ref, a_ref, b_ref, state_in, *rest):
    if last:
        keep_ref, send_ref, start_ref, kx_ref, vx_ref, kp_ref, state_ref = rest
    else:
        state_ref, done_ref, start_ref, kx_ref, vx_ref, kp_ref = rest
        done_ref[...] = jnp.zeros(done_ref.shape, jnp.float32)
    keys = kp_ref.shape[0]
    chip_row, core, block, ends = place_of(hop, keys, docs_ref)
    first = hop == 1
    first_start = starts_of(chip_row, ends)
    active = block + keys > first_start
    if first:
        state_ref[...] = state_in[...]
    else:

        @pl.when(jnp.logical_not(active))
        def _():
            state_ref[...] = state_in[...]

    @pl.when(active)
    def _():
        lay_keys(a_ref, b_ref, kx_ref, vx_ref)
        if first:

            @pl.when(block + keys == chip_row)
            def _():
                near(
                    [keys], chip_row, block, ends, taps_ref, qp_ref, kx_ref, vx_ref, start_ref,
                    state_ref,
                )

        convolve(False, block, first_start, ends, qp_ref, kx_ref, kp_ref)
        source = state_ref if first else state_in
        far(2 if last else 4, chip_row, block, ends, qp_ref, kp_ref, vx_ref, source, state_ref)

    if last:
        for ref, side in ((keep_ref, core), (send_ref, 1 - core)):
            ref[...] = state_ref[pl.ds(pl.multiple_of(side * keys, keys), keys), :]


def join_kernel(keep_ref, other_ref, own_ref, cross_ref):
    wide = 2 * HEAD_DIM
    stats, more = keep_ref[:, wide:], other_ref[:, wide:]
    m_a, l_a = stats[:, 0:1], stats[:, 64:65]
    m_b, l_b = more[:, 0:1], more[:, 64:65]
    m = jnp.maximum(m_a, m_b)
    f_a, f_b = jnp.exp(m_a - m), jnp.exp(m_b - m)
    share = 1.0 / (l_a * f_a + l_b * f_b)
    f_a, f_b = f_a * share, f_b * share
    own_ref[...] = keep_ref[:, :HEAD_DIM] * f_a + other_ref[:, :HEAD_DIM] * f_b
    cross_ref[...] = (
        keep_ref[:, HEAD_DIM:wide] * f_a + other_ref[:, HEAD_DIM:wide] * f_b
    ).astype(jnp.bfloat16)


def finish_kernel(mixing_ref, own_ref, cross_ref, gain_ref, out_ref):
    mixed = mixing_ref[0] * own_ref[...] + mixing_ref[1] * cross_ref[...].astype(jnp.float32)
    mean = jnp.mean(mixed * mixed, axis=1, keepdims=True)
    out_ref[...] = (mixed * lax.rsqrt(mean + 1e-05) * gain_ref[...]).astype(jnp.bfloat16)


VMEM = pl.BlockSpec(memory_space=pltpu.VMEM)
SMEM = pl.BlockSpec(memory_space=pltpu.SMEM)


def call(kernel, specs, out, scratch, args, flops=0):
    shapes = [jax.ShapeDtypeStruct(shape, dtype) for shape, dtype in out]
    return pl.pallas_call(
        kernel,
        out_shape=shapes,
        in_specs=specs,
        out_specs=[VMEM] * len(shapes),
        scratch_shapes=scratch,
        cost_estimate=pl.CostEstimate(flops=8 * flops, bytes_accessed=4 << 20, transcendentals=0),
        compiler_params=pltpu.CompilerParams(vmem_limit_bytes=20 << 20),
    )(*args)


def body(queries, key_vectors, values, kernel, mixing, norm_gain, doc_lengths):
    rows = queries.shape[0]
    bf16, f32 = jnp.bfloat16, jnp.float32
    count = lax.axis_size("ctx")
    heads = lax.axis_size("head")
    taps = kernel.shape[1]
    width = taps * HEAD_DIM

    def permute(value, pairs):
        return lax.ppermute(value, "ctx", pairs)

    def onward(value):
        return permute(value, [(i, (i + 2) % count) for i in range(count)])

    def partner(value):
        return lax.ppermute(value, "head", [(i, i ^ (heads // 2)) for i in range(heads)])

    def step(value, by):
        return permute(value, [(i, (i + by) % count) for i in range(count)])

    other_values = partner(values)
    beyond = step(key_vectors[:HALO], -1)
    behind = step(jnp.concatenate([key_vectors[rows - HALO :], queries[rows - HALO :]]), 1)
    mine = jnp.concatenate([queries, behind[HALO:]])
    sibling = permute(mine, [(i, i ^ 1) for i in range(count)])
    by_tap = jnp.transpose(kernel, (1, 0, 2))
    ring_a = key_vectors
    ring_b = jnp.concatenate([values, other_values, behind[:HALO], beyond])
    state = [((2 * rows, 3 * HEAD_DIM), f32)]
    mark = [((8, 128), f32)]
    scratch = [
        pltpu.VMEM((TILES, BAND // 2 + 8, GROUP), jnp.int32),
        pltpu.VMEM((rows + 128, HEAD_DIM), bf16),
        pltpu.VMEM((rows + 128, 2 * HEAD_DIM), bf16),
        pltpu.VMEM((rows, 2 * width), bf16),
    ]
    flops = 2 * 2 * rows * rows * (2 * width + 2 * HEAD_DIM)
    operand, running, done = call(
        local_kernel,
        [SMEM, SMEM, VMEM, VMEM, VMEM, pl.BlockSpec(memory_space=pltpu.HBM), VMEM],
        [((2 * rows + 2 * taps * GROUP * 256 // width, width), bf16)]
        + state
        + mark,
        [pltpu.VMEM((2 * rows + HALO, HEAD_DIM), f32), pltpu.SemaphoreType.DMA] + scratch,
        (doc_lengths, by_tap, mine, sibling, behind, ring_a, ring_b),
        flops=8 * flops,
    )
    for hop in range(1, HOPS + 1):
        ring_a, ring_b = onward(ring_a), onward(ring_b)
        ring_a, _ = lax.optimization_barrier((ring_a, done))
        ring_b, _ = lax.optimization_barrier((ring_b, done))
        last = hop == HOPS
        out = [((rows, 3 * HEAD_DIM), f32)] * 2 if last else state + mark
        extra = [pltpu.VMEM(shape, dtype) for shape, dtype in state] if last else []
        result = call(
            functools.partial(hop_kernel, hop, last),
            [SMEM, SMEM] + [VMEM] * 4,
            out,
            scratch + extra,
            (doc_lengths, by_tap, operand, ring_a, ring_b, running),
            flops=8 * flops,
        )
        if not last:
            running, done = result
    keep, send = result
    other = permute(send, [(i, i ^ 1) for i in range(count)])
    own, cross = call(
        join_kernel,
        [VMEM, VMEM],
        [((rows, HEAD_DIM), f32), ((rows, HEAD_DIM), bf16)],
        [],
        (keep, other),
    )
    (finished,) = call(
        finish_kernel,
        [SMEM, VMEM, VMEM, VMEM],
        [((rows, HEAD_DIM), bf16)],
        [],
        (mixing.reshape(-1), own, partner(cross), norm_gain.reshape(1, HEAD_DIM)),
    )
    return finished


def solution(mesh):
    return jax.shard_map(
        body,
        mesh=mesh,
        in_specs=(
            P("ctx", "head"),
            P("ctx", "head"),
            P("ctx", "head"),
            P("head", None, None),
            P("head", None),
            P("head"),
            P(),
        ),
        out_specs=P("ctx", "head"),
        check_vma=False,
    )
```

```python
import functools

import jax
import jax.numpy as jnp
from jax import lax
from jax.experimental import pallas as pl
from jax.experimental.pallas import tpu as pltpu
from jax.sharding import PartitionSpec as P

HEAD_DIM = 128
SCALE = HEAD_DIM ** (-0.5)
MASKED = -1e30
FLOOR = -1e20
HALO = 16
BAND = 64
TILES = 4
GROUP = 128
WIDE = 256
REACH = 10
HOPS = 4


def dot(a, b):
    return lax.dot_general(a, b, (((1,), (0,)), ((), ())), preferred_element_type=jnp.float32)


def dot_t(a, b):
    return lax.dot_general(a, b, (((1,), (1,)), ((), ())), preferred_element_type=jnp.float32)


def starts_of(position, ends):
    start = jnp.zeros_like(position)
    for end in ends:
        start = jnp.where(position >= end, end, start)
    return start


def widen(column, times):
    return jnp.concatenate([column] * times, axis=1) if times > 1 else column


def absorb(tiles, source_ref, state_ref):
    wide = 2 * HEAD_DIM
    done = []
    for rows, logits, values in tiles:
        m_old = source_ref[rows, wide : wide + 1]
        m_new = jnp.maximum(m_old, jnp.max(logits, axis=1, keepdims=True))
        weights = jnp.exp(logits - m_new)
        factor = jnp.exp(m_old - m_new)
        total = source_ref[rows, wide + 64 : wide + 65] * factor
        total = total + jnp.sum(weights, axis=1, keepdims=True)
        product = dot(weights.astype(jnp.bfloat16), values)
        product = source_ref[rows, 0:wide] * factor + product
        lane = lax.broadcasted_iota(jnp.int32, (logits.shape[0], 128), 1)
        done.append((rows, jnp.where(lane < 64, m_new, total), product))
    for rows, stats, product in done:
        state_ref[rows, 0:wide] = product
        state_ref[rows, wide:] = stats


def taps_at(qp_ref, rest, u):
    most = qp_ref.shape[1] // 256
    sets = qp_ref.shape[1] // HEAD_DIM // most
    row = qp_ref.shape[0] - (2 - rest) * sets * GROUP + u // most * GROUP
    return slice(row, row + GROUP), slice(u % most * 256, u % most * 256 + 256)


def lay_keys(a_ref, b_ref, kx_ref, vx_ref):
    keys = kx_ref.shape[0] - 128
    kx_ref[0:HALO, :] = b_ref[2 * keys : 2 * keys + HALO, :]
    if a_ref is not None:
        kx_ref[HALO : HALO + keys, :] = a_ref[...]
    kx_ref[HALO + keys : 2 * HALO + keys, :] = b_ref[2 * keys + HALO :, :]
    kx_ref[2 * HALO + keys :, :] = jnp.zeros_like(kx_ref[2 * HALO + keys :, :])
    vx_ref[0:HALO, :] = jnp.zeros((HALO, 2 * HEAD_DIM), jnp.bfloat16)
    vx_ref[HALO : HALO + keys, 0:HEAD_DIM] = b_ref[0:keys, :]
    vx_ref[HALO : HALO + keys, HEAD_DIM:] = b_ref[keys : 2 * keys, :]
    vx_ref[HALO + keys :, :] = jnp.zeros_like(vx_ref[HALO + keys :, :])


def near(tiles, chip_row, block, ends, taps_ref, qp_ref, kx_ref, vx_ref, start_ref, state_ref):
    keys = kx_ref.shape[0] - 128
    query_taps, _, key_taps = taps_ref.shape
    rim = (key_taps - 1) // 2
    half = BAND // 2
    shape = (half, GROUP)
    for n, a in enumerate(tiles):
        top = block + a
        one_start = starts_of(top + BAND - 1, ends)
        one = starts_of(top - 8, ends) == one_start

        @pl.when(one)
        def _(n=n, one_start=one_start):
            start_ref[n] = jnp.full(start_ref.shape[1:], one_start, jnp.int32)

        @pl.when(jnp.logical_not(one))
        def _(n=n, top=top):
            side = lax.broadcasted_iota(jnp.int32, start_ref.shape[1:], 1) >= 64
            position = top - 8 + lax.broadcasted_iota(jnp.int32, start_ref.shape[1:], 0)
            start_ref[n] = starts_of(position + jnp.where(side, half, 0), ends)

    lane = lax.broadcasted_iota(jnp.int32, shape, 1)
    left = lane < 64
    shift = jnp.where(left, 0, half)
    step = lax.broadcasted_iota(jnp.int32, shape, 0) + shift
    place = lane - HALO - shift
    behind = step - place
    work = []
    for n, a in enumerate(tiles):
        rows = pl.ds(pl.multiple_of(block - chip_row + a, 16), BAND)
        parts = [
            (pl.ds(pl.multiple_of(a + m, 16), 64), pl.ds(pl.multiple_of(block - chip_row + a + m, 16), half))
            for m in (0, half)
        ]
        stacked = jnp.concatenate(
            [
                qp_ref[part, u * HEAD_DIM : (u + 1) * HEAD_DIM]
                for _, part in parts
                for u in range(query_taps)
            ],
            axis=0,
        )
        window = jnp.concatenate([kx_ref[span, :] for span, _ in parts], axis=0)
        values = jnp.concatenate([vx_ref[span, :] for span, _ in parts], axis=0)
        work.append((n, rows, block + a + place, dot_t(stacked, window), values))
    done = []
    for n, rows, col, products, values in work:
        scores = []
        for u in range(query_taps):
            both = [products[(m * query_taps + u) * half :][:half] for m in (0, 1)]
            allowed = (behind >= u) & (col >= start_ref[n, 8 - u : 8 - u + half, :])
            scores.append(jnp.where(allowed, jnp.where(left, *both), 0.0))
        conv = None
        for t in range(key_taps):
            terms = None
            for u in range(query_taps):
                tap = taps_ref[u, 0, t] * SCALE
                if u == 0 and t == rim:
                    tap = tap + SCALE
                terms = scores[u] * tap if terms is None else terms + scores[u] * tap
            if t != rim:
                terms = pltpu.roll(terms, (t - rim) % GROUP, 1)
            conv = terms if conv is None else conv + terms
        inside = (col >= block) & (col < block + keys) & (col >= start_ref[n, 8 : 8 + half, :])
        inside = inside & (behind >= 0) & (behind < REACH)
        logits = jnp.concatenate(
            [
                jnp.where(inside & left, conv, MASKED),
                jnp.where(inside & jnp.logical_not(left), conv, MASKED),
            ],
            axis=0,
        )
        done.append((rows, logits, values))
    absorb(done, state_ref, state_ref)


def convolve(local, block, first_start, ends, qp_ref, kx_ref, kp_ref):
    total = kx_ref.shape[0]
    keys = kp_ref.shape[0]
    width = kp_ref.shape[1] // 2
    taps = width // HEAD_DIM
    depth = 256
    def put(g, u, done):
        top = done.astype(jnp.bfloat16)
        rest = (done - top.astype(jnp.float32)).astype(jnp.bfloat16)
        for n in range(done.shape[1] // HEAD_DIM):
            here = slice((g + n) * GROUP, (g + n + 1) * GROUP)
            lanes = slice(n * HEAD_DIM, (n + 1) * HEAD_DIM)
            kp_ref[here, u * HEAD_DIM : (u + 1) * HEAD_DIM] = top[:, lanes]
            kp_ref[here, width + u * HEAD_DIM : width + (u + 1) * HEAD_DIM] = rest[:, lanes]

    def whole():
        for g in range(0, keys // GROUP, 2):
            window = jnp.concatenate(
                [kx_ref[n * GROUP : n * GROUP + depth, :] for n in (g, g + 1)], axis=1
            )
            for u in range(taps):
                high, rest = (qp_ref[taps_at(qp_ref, n, u)] for n in (0, 1))
                put(g, u, dot(high, window) + dot(rest, window))

    def cut():
        for g in range(keys // GROUP):
            shape = (GROUP, depth)
            out = block + g * GROUP + lax.broadcasted_iota(jnp.int32, shape, 0)
            inp = block + g * GROUP - HALO + lax.broadcasted_iota(jnp.int32, shape, 1)
            keep = inp >= starts_of(out, ends)
            window = kx_ref[g * GROUP : g * GROUP + depth, :]
            for u in range(taps):
                high, rest = (
                    jnp.where(keep, qp_ref[taps_at(qp_ref, n, u)].astype(jnp.float32), 0.0).astype(
                        jnp.bfloat16
                    )
                    for n in (0, 1)
                )
                put(g, u, dot(high, window) + dot(rest, window))

    if local:
        unbroken = starts_of(block + keys - 1, ends) <= block - HALO

        @pl.when(unbroken)
        def _():
            whole()

        @pl.when(jnp.logical_not(unbroken))
        def _():
            cut()

        return
    place = block - HALO + lax.broadcasted_iota(jnp.int32, (total, HEAD_DIM), 0)
    kx_ref[...] = jnp.where(place >= first_start, kx_ref[...].astype(jnp.float32), 0.0).astype(
        jnp.bfloat16
    )
    whole()


def far(tiles_at_once, chip_row, block, ends, qp_ref, kp_ref, vx_ref, source_ref, state_ref):
    keys = kp_ref.shape[0]
    width = qp_ref.shape[1]
    span = tiles_at_once * WIDE

    @pl.loop(0, state_ref.shape[0] // span)
    def _(tile):
        first = tile * span
        top = chip_row + first
        needed = (top + span - 1 >= block + REACH) & (block + keys > starts_of(top, ends))

        @pl.when(needed)
        def _():
            tiles = []
            shape = (WIDE, GROUP)
            col = lax.broadcasted_iota(jnp.int32, (WIDE, keys), 1)
            for half in range(0, span, WIDE):
                rows = pl.ds(pl.multiple_of(first + half, WIDE), WIDE)
                query = qp_ref[rows, :]
                conv = dot_t(query, kp_ref[:, 0:width]) + dot_t(query, kp_ref[:, width:])
                row = top + half + lax.broadcasted_iota(jnp.int32, shape, 0)
                start = widen(starts_of(row, ends) - block, keys // GROUP)
                row = widen(row - (REACH + block), keys // GROUP)
                logits = jnp.where((col <= row) & (col >= start), conv, MASKED)
                tiles.append((rows, logits, vx_ref[HALO : HALO + keys, :]))
            absorb(tiles, source_ref, state_ref)

        if source_ref is not state_ref:

            @pl.when(jnp.logical_not(needed))
            def _():
                rows = pl.ds(pl.multiple_of(first, WIDE), span)
                state_ref[rows, :] = source_ref[rows, :]


def place_of(hop, rows, docs_ref):
    group = lax.axis_index("ctx")
    core = group & 1
    chip = group >> 1
    ends = [docs_ref[0]]
    for d in range(1, 7):
        ends.append(ends[-1] + docs_ref[d])
    return chip * 2 * rows, core, (chip - hop) * 2 * rows + core * rows, ends


def local_kernel(
    docs_ref, taps_ref, own_ref, other_ref, edge_ref, a_ref, b_ref,
    qp_ref, state_ref, done_ref,
    qx_ref, copied, start_ref, kx_ref, vx_ref, kp_ref,
):
    keys = kp_ref.shape[0]
    chip_row, core, block, ends = place_of(0, keys, docs_ref)
    taken = pltpu.make_async_copy(a_ref, kx_ref.at[pl.ds(HALO, keys), :], copied)
    taken.start()
    taps, _, key_taps = taps_ref.shape
    rim = (key_taps - 1) // 2
    done_ref[...] = jnp.zeros(done_ref.shape, jnp.float32)

    @pl.when(core == 0)
    def _():
        qx_ref[0:HALO, :] = edge_ref[HALO:, :].astype(jnp.float32)
        qx_ref[HALO : HALO + keys, :] = own_ref[0:keys, :].astype(jnp.float32)
        qx_ref[HALO + keys :, :] = other_ref[0:keys, :].astype(jnp.float32)

    @pl.when(core != 0)
    def _():
        qx_ref[0:HALO, :] = other_ref[keys:, :].astype(jnp.float32)
        qx_ref[HALO : HALO + keys, :] = other_ref[0:keys, :].astype(jnp.float32)
        qx_ref[HALO + keys :, :] = own_ref[0:keys, :].astype(jnp.float32)

    count = state_ref.shape[0]
    for u in range(taps):
        qp_ref[0:count, u * HEAD_DIM : (u + 1) * HEAD_DIM] = qx_ref[
            HALO - u : HALO - u + count, :
        ].astype(jnp.bfloat16)
    lane = lax.broadcasted_iota(jnp.int32, (8, 256), 1)
    for u in range(taps):
        base = jnp.zeros(lane.shape, jnp.float32)
        for t in range(key_taps):
            tap = taps_ref[u, 0, t] * SCALE
            if u == 0 and t == rim:
                tap = tap + SCALE
            base = jnp.where(lane == HALO + rim - t, tap, base)
        band = jnp.concatenate([base] * (GROUP // 8), axis=0)
        band = pltpu.roll(band, 0, 1, stride=1, stride_axis=0)
        high = band.astype(jnp.bfloat16)
        qp_ref[taps_at(qp_ref, 0, u)] = high
        qp_ref[taps_at(qp_ref, 1, u)] = (band - high.astype(jnp.float32)).astype(jnp.bfloat16)
    lane = lax.broadcasted_iota(jnp.int32, (count, 128), 1)
    state_ref[:, 0 : 2 * HEAD_DIM] = jnp.zeros((count, 2 * HEAD_DIM), jnp.float32)
    state_ref[:, 2 * HEAD_DIM :] = jnp.where(lane < 64, FLOOR, 0.0)
    lay_keys(None, b_ref, kx_ref, vx_ref)
    taken.wait()
    rest = (chip_row, block, ends, taps_ref, qp_ref, kx_ref, vx_ref, start_ref, state_ref)

    tiles = [n * BAND for n in range(keys // BAND)]
    past = block + keys - chip_row < count
    near(tiles[:TILES], *rest)

    @pl.when(past)
    def _():
        near(tiles[TILES:] + [keys], *rest)

    @pl.when(jnp.logical_not(past))
    def _():
        near(tiles[TILES:], *rest)

    convolve(True, block, 0, ends, qp_ref, kx_ref, kp_ref)
    far(4, chip_row, block, ends, qp_ref, kp_ref, vx_ref, state_ref, state_ref)


def hop_kernel(hop, last, docs_ref, taps_ref, qp_ref, a_ref, b_ref, state_in, *rest):
    if last:
        keep_ref, send_ref, start_ref, kx_ref, vx_ref, kp_ref, state_ref = rest
    else:
        state_ref, done_ref, start_ref, kx_ref, vx_ref, kp_ref = rest
        done_ref[...] = jnp.zeros(done_ref.shape, jnp.float32)
    keys = kp_ref.shape[0]
    chip_row, core, block, ends = place_of(hop, keys, docs_ref)
    first = hop == 1
    first_start = starts_of(chip_row, ends)
    active = block + keys > first_start
    if first:
        state_ref[...] = state_in[...]
    else:

        @pl.when(jnp.logical_not(active))
        def _():
            state_ref[...] = state_in[...]

    @pl.when(active)
    def _():
        lay_keys(a_ref, b_ref, kx_ref, vx_ref)
        if first:

            @pl.when(block + keys == chip_row)
            def _():
                near(
                    [keys], chip_row, block, ends, taps_ref, qp_ref, kx_ref, vx_ref, start_ref,
                    state_ref,
                )

        convolve(False, block, first_start, ends, qp_ref, kx_ref, kp_ref)
        source = state_ref if first else state_in
        far(2 if last else 4, chip_row, block, ends, qp_ref, kp_ref, vx_ref, source, state_ref)

    if last:
        for ref, side in ((keep_ref, core), (send_ref, 1 - core)):
            ref[...] = state_ref[pl.ds(pl.multiple_of(side * keys, keys), keys), :]


def join_kernel(keep_ref, other_ref, own_ref, cross_ref):
    wide = 2 * HEAD_DIM
    stats, more = keep_ref[:, wide:], other_ref[:, wide:]
    m_a, l_a = stats[:, 0:1], stats[:, 64:65]
    m_b, l_b = more[:, 0:1], more[:, 64:65]
    m = jnp.maximum(m_a, m_b)
    f_a, f_b = jnp.exp(m_a - m), jnp.exp(m_b - m)
    share = 1.0 / (l_a * f_a + l_b * f_b)
    f_a, f_b = f_a * share, f_b * share
    own_ref[...] = keep_ref[:, :HEAD_DIM] * f_a + other_ref[:, :HEAD_DIM] * f_b
    cross_ref[...] = (
        keep_ref[:, HEAD_DIM:wide] * f_a + other_ref[:, HEAD_DIM:wide] * f_b
    ).astype(jnp.bfloat16)


def finish_kernel(mixing_ref, own_ref, cross_ref, gain_ref, out_ref):
    mixed = mixing_ref[0] * own_ref[...] + mixing_ref[1] * cross_ref[...].astype(jnp.float32)
    mean = jnp.mean(mixed * mixed, axis=1, keepdims=True)
    out_ref[...] = (mixed * lax.rsqrt(mean + 1e-05) * gain_ref[...]).astype(jnp.bfloat16)


VMEM = pl.BlockSpec(memory_space=pltpu.VMEM)
SMEM = pl.BlockSpec(memory_space=pltpu.SMEM)


def call(kernel, specs, out, scratch, args, flops=0):
    shapes = [jax.ShapeDtypeStruct(shape, dtype) for shape, dtype in out]
    return pl.pallas_call(
        kernel,
        out_shape=shapes,
        in_specs=specs,
        out_specs=[VMEM] * len(shapes),
        scratch_shapes=scratch,
        cost_estimate=pl.CostEstimate(flops=8 * flops, bytes_accessed=4 << 20, transcendentals=0),
        compiler_params=pltpu.CompilerParams(vmem_limit_bytes=20 << 20),
    )(*args)


def body(queries, key_vectors, values, kernel, mixing, norm_gain, doc_lengths):
    rows = queries.shape[0]
    bf16, f32 = jnp.bfloat16, jnp.float32
    count = lax.axis_size("ctx")
    heads = lax.axis_size("head")
    taps = kernel.shape[1]
    width = taps * HEAD_DIM

    def permute(value, pairs):
        return lax.ppermute(value, "ctx", pairs)

    def onward(value):
        return permute(value, [(i, (i + 2) % count) for i in range(count)])

    def partner(value):
        return lax.ppermute(value, "head", [(i, i ^ (heads // 2)) for i in range(heads)])

    def step(value, by):
        return permute(value, [(i, (i + by) % count) for i in range(count)])

    other_values = partner(values)
    beyond = step(key_vectors[:HALO], -1)
    behind = step(jnp.concatenate([key_vectors[rows - HALO :], queries[rows - HALO :]]), 1)
    mine = jnp.concatenate([queries, behind[HALO:]])
    sibling = permute(mine, [(i, i ^ 1) for i in range(count)])
    by_tap = jnp.transpose(kernel, (1, 0, 2))
    ring_a = key_vectors
    ring_b = jnp.concatenate([values, other_values, behind[:HALO], beyond])
    state = [((2 * rows, 3 * HEAD_DIM), f32)]
    mark = [((8, 128), f32)]
    scratch = [
        pltpu.VMEM((TILES + 1, BAND // 2 + 8, GROUP), jnp.int32),
        pltpu.VMEM((rows + 128, HEAD_DIM), bf16),
        pltpu.VMEM((rows + 128, 2 * HEAD_DIM), bf16),
        pltpu.VMEM((rows, 2 * width), bf16),
    ]
    flops = 2 * 2 * rows * rows * (2 * width + 2 * HEAD_DIM)
    operand, running, done = call(
        local_kernel,
        [SMEM, SMEM, VMEM, VMEM, VMEM, pl.BlockSpec(memory_space=pltpu.HBM), VMEM],
        [((2 * rows + 2 * taps * GROUP * 256 // width, width), bf16)]
        + state
        + mark,
        [pltpu.VMEM((2 * rows + HALO, HEAD_DIM), f32), pltpu.SemaphoreType.DMA] + scratch,
        (doc_lengths, by_tap, mine, sibling, behind, ring_a, ring_b),
        flops=8 * flops,
    )
    for hop in range(1, HOPS + 1):
        ring_a, ring_b = onward(ring_a), onward(ring_b)
        ring_a, _ = lax.optimization_barrier((ring_a, done))
        ring_b, _ = lax.optimization_barrier((ring_b, done))
        last = hop == HOPS
        out = [((rows, 3 * HEAD_DIM), f32)] * 2 if last else state + mark
        extra = [pltpu.VMEM(shape, dtype) for shape, dtype in state] if last else []
        result = call(
            functools.partial(hop_kernel, hop, last),
            [SMEM, SMEM] + [VMEM] * 4,
            out,
            scratch + extra,
            (doc_lengths, by_tap, operand, ring_a, ring_b, running),
            flops=8 * flops,
        )
        if not last:
            running, done = result
    keep, send = result
    other = permute(send, [(i, i ^ 1) for i in range(count)])
    own, cross = call(
        join_kernel,
        [VMEM, VMEM],
        [((rows, HEAD_DIM), f32), ((rows, HEAD_DIM), bf16)],
        [],
        (keep, other),
    )
    (finished,) = call(
        finish_kernel,
        [SMEM, VMEM, VMEM, VMEM],
        [((rows, HEAD_DIM), bf16)],
        [],
        (mixing.reshape(-1), own, partner(cross), norm_gain.reshape(1, HEAD_DIM)),
    )
    return finished


def solution(mesh):
    return jax.shard_map(
        body,
        mesh=mesh,
        in_specs=(
            P("ctx", "head"),
            P("ctx", "head"),
            P("ctx", "head"),
            P("head", None, None),
            P("head", None),
            P("head"),
            P(),
        ),
        out_specs=P("ctx", "head"),
        check_vma=False,
    )
```

```python
import functools

import jax
import jax.numpy as jnp
from jax import lax
from jax.experimental import pallas as pl
from jax.experimental.pallas import tpu as pltpu
from jax.sharding import PartitionSpec as P

HEAD_DIM = 128
SCALE = HEAD_DIM ** (-0.5)
MASKED = -1e30
FLOOR = -1e20
HALO = 16
BAND = 64
TILES = 4
GROUP = 128
WIDE = 256
REACH = 10
HOPS = 4


def dot(a, b):
    return lax.dot_general(a, b, (((1,), (0,)), ((), ())), preferred_element_type=jnp.float32)


def dot_t(a, b):
    return lax.dot_general(a, b, (((1,), (1,)), ((), ())), preferred_element_type=jnp.float32)


def starts_of(position, ends):
    start = jnp.zeros_like(position)
    for end in ends:
        start = jnp.where(position >= end, end, start)
    return start


def widen(column, times):
    return jnp.concatenate([column] * times, axis=1) if times > 1 else column


def absorb(tiles, source_ref, state_ref):
    wide = 2 * HEAD_DIM
    done = []
    for rows, logits, values in tiles:
        m_old = source_ref[rows, wide : wide + 1]
        m_new = jnp.maximum(m_old, jnp.max(logits, axis=1, keepdims=True))
        weights = jnp.exp(logits - m_new)
        factor = jnp.exp(m_old - m_new)
        total = source_ref[rows, wide + 64 : wide + 65] * factor
        total = total + jnp.sum(weights, axis=1, keepdims=True)
        product = dot(weights.astype(jnp.bfloat16), values)
        product = source_ref[rows, 0:wide] * factor + product
        lane = lax.broadcasted_iota(jnp.int32, (logits.shape[0], 128), 1)
        done.append((rows, jnp.where(lane < 64, m_new, total), product))
    for rows, stats, product in done:
        state_ref[rows, 0:wide] = product
        state_ref[rows, wide:] = stats


def taps_at(qp_ref, rest, u):
    most = qp_ref.shape[1] // 256
    sets = qp_ref.shape[1] // HEAD_DIM // most
    row = qp_ref.shape[0] - (2 - rest) * sets * GROUP + u // most * GROUP
    return slice(row, row + GROUP), slice(u % most * 256, u % most * 256 + 256)


def lay_keys(a_ref, b_ref, kx_ref, vx_ref):
    keys = kx_ref.shape[0] - 128
    kx_ref[0:HALO, :] = b_ref[2 * keys : 2 * keys + HALO, :]
    if a_ref is not None:
        kx_ref[HALO : HALO + keys, :] = a_ref[...]
    kx_ref[HALO + keys : 2 * HALO + keys, :] = b_ref[2 * keys + HALO :, :]
    kx_ref[2 * HALO + keys :, :] = jnp.zeros_like(kx_ref[2 * HALO + keys :, :])
    vx_ref[0:HALO, :] = jnp.zeros((HALO, 2 * HEAD_DIM), jnp.bfloat16)
    vx_ref[HALO : HALO + keys, 0:HEAD_DIM] = b_ref[0:keys, :]
    vx_ref[HALO : HALO + keys, HEAD_DIM:] = b_ref[keys : 2 * keys, :]
    vx_ref[HALO + keys :, :] = jnp.zeros_like(vx_ref[HALO + keys :, :])


def near(tiles, chip_row, block, ends, taps_ref, qp_ref, kx_ref, vx_ref, start_ref, state_ref):
    keys = kx_ref.shape[0] - 128
    query_taps, _, key_taps = taps_ref.shape
    rim = (key_taps - 1) // 2
    half = BAND // 2
    shape = (half, GROUP)
    for n, a in enumerate(tiles):
        top = block + a
        one_start = starts_of(top + BAND - 1, ends)
        one = starts_of(top - 8, ends) == one_start

        @pl.when(one)
        def _(n=n, one_start=one_start):
            start_ref[n] = jnp.full(start_ref.shape[1:], one_start, jnp.int32)

        @pl.when(jnp.logical_not(one))
        def _(n=n, top=top):
            side = lax.broadcasted_iota(jnp.int32, start_ref.shape[1:], 1) >= 64
            position = top - 8 + lax.broadcasted_iota(jnp.int32, start_ref.shape[1:], 0)
            start_ref[n] = starts_of(position + jnp.where(side, half, 0), ends)

    lane = lax.broadcasted_iota(jnp.int32, shape, 1)
    left = lane < 64
    shift = jnp.where(left, 0, half)
    step = lax.broadcasted_iota(jnp.int32, shape, 0) + shift
    place = lane - HALO - shift
    behind = step - place
    work = []
    for n, a in enumerate(tiles):
        rows = pl.ds(pl.multiple_of(block - chip_row + a, 16), BAND)
        parts = [
            (pl.ds(pl.multiple_of(a + m, 16), 64), pl.ds(pl.multiple_of(block - chip_row + a + m, 16), half))
            for m in (0, half)
        ]
        stacked = jnp.concatenate(
            [
                qp_ref[part, u * HEAD_DIM : (u + 1) * HEAD_DIM]
                for _, part in parts
                for u in range(query_taps)
            ],
            axis=0,
        )
        window = jnp.concatenate([kx_ref[span, :] for span, _ in parts], axis=0)
        values = jnp.concatenate([vx_ref[span, :] for span, _ in parts], axis=0)
        work.append((n, rows, block + a + place, dot_t(stacked, window), values))
    done = []
    for n, rows, col, products, values in work:
        scores = []
        for u in range(query_taps):
            both = [products[(m * query_taps + u) * half :][:half] for m in (0, 1)]
            allowed = (behind >= u) & (col >= start_ref[n, 8 - u : 8 - u + half, :])
            scores.append(jnp.where(allowed, jnp.where(left, *both), 0.0))
        conv = None
        for t in range(key_taps):
            terms = None
            for u in range(query_taps):
                tap = taps_ref[u, 0, t] * SCALE
                if u == 0 and t == rim:
                    tap = tap + SCALE
                terms = scores[u] * tap if terms is None else terms + scores[u] * tap
            if t != rim:
                terms = pltpu.roll(terms, (t - rim) % GROUP, 1)
            conv = terms if conv is None else conv + terms
        inside = (col >= block) & (col < block + keys) & (col >= start_ref[n, 8 : 8 + half, :])
        inside = inside & (behind >= 0) & (behind < REACH)
        logits = jnp.concatenate(
            [
                jnp.where(inside & left, conv, MASKED),
                jnp.where(inside & jnp.logical_not(left), conv, MASKED),
            ],
            axis=0,
        )
        done.append((rows, logits, values))
    absorb(done, state_ref, state_ref)


def convolve(local, block, first_start, ends, qp_ref, kx_ref, kp_ref):
    total = kx_ref.shape[0]
    keys = kp_ref.shape[0]
    width = kp_ref.shape[1] // 2
    taps = width // HEAD_DIM
    depth = 256
    def put(g, u, done):
        top = done.astype(jnp.bfloat16)
        rest = (done - top.astype(jnp.float32)).astype(jnp.bfloat16)
        for n in range(done.shape[1] // HEAD_DIM):
            here = slice((g + n) * GROUP, (g + n + 1) * GROUP)
            lanes = slice(n * HEAD_DIM, (n + 1) * HEAD_DIM)
            kp_ref[here, u * HEAD_DIM : (u + 1) * HEAD_DIM] = top[:, lanes]
            kp_ref[here, width + u * HEAD_DIM : width + (u + 1) * HEAD_DIM] = rest[:, lanes]

    def whole():
        for g in range(0, keys // GROUP, 2):
            window = jnp.concatenate(
                [kx_ref[n * GROUP : n * GROUP + depth, :] for n in (g, g + 1)], axis=1
            )
            for u in range(taps):
                high, rest = (qp_ref[taps_at(qp_ref, n, u)] for n in (0, 1))
                put(g, u, dot(high, window) + dot(rest, window))

    def cut():
        for g in range(keys // GROUP):
            shape = (GROUP, depth)
            out = block + g * GROUP + lax.broadcasted_iota(jnp.int32, shape, 0)
            inp = block + g * GROUP - HALO + lax.broadcasted_iota(jnp.int32, shape, 1)
            keep = inp >= starts_of(out, ends)
            window = kx_ref[g * GROUP : g * GROUP + depth, :]
            for u in range(taps):
                high, rest = (
                    jnp.where(keep, qp_ref[taps_at(qp_ref, n, u)].astype(jnp.float32), 0.0).astype(
                        jnp.bfloat16
                    )
                    for n in (0, 1)
                )
                put(g, u, dot(high, window) + dot(rest, window))

    if local:
        unbroken = starts_of(block + keys - 1, ends) <= block - HALO

        @pl.when(unbroken)
        def _():
            whole()

        @pl.when(jnp.logical_not(unbroken))
        def _():
            cut()

        return
    place = block - HALO + lax.broadcasted_iota(jnp.int32, (total, HEAD_DIM), 0)
    kx_ref[...] = jnp.where(place >= first_start, kx_ref[...].astype(jnp.float32), 0.0).astype(
        jnp.bfloat16
    )
    whole()


def far(tiles_at_once, chip_row, block, ends, qp_ref, kp_ref, vx_ref, source_ref, state_ref):
    keys = kp_ref.shape[0]
    width = qp_ref.shape[1]
    span = tiles_at_once * WIDE

    @pl.loop(0, state_ref.shape[0] // span)
    def _(tile):
        first = tile * span
        top = chip_row + first
        needed = (top + span - 1 >= block + REACH) & (block + keys > starts_of(top, ends))

        @pl.when(needed)
        def _():
            tiles = []
            shape = (WIDE, GROUP)
            col = lax.broadcasted_iota(jnp.int32, (WIDE, keys), 1)
            for half in range(0, span, WIDE):
                rows = pl.ds(pl.multiple_of(first + half, WIDE), WIDE)
                query = qp_ref[rows, :]
                conv = dot_t(query, kp_ref[:, 0:width]) + dot_t(query, kp_ref[:, width:])
                row = top + half + lax.broadcasted_iota(jnp.int32, shape, 0)
                start = widen(starts_of(row, ends) - block, keys // GROUP)
                row = widen(row - (REACH + block), keys // GROUP)
                logits = jnp.where((col <= row) & (col >= start), conv, MASKED)
                tiles.append((rows, logits, vx_ref[HALO : HALO + keys, :]))
            absorb(tiles, source_ref, state_ref)

        if source_ref is not state_ref:

            @pl.when(jnp.logical_not(needed))
            def _():
                rows = pl.ds(pl.multiple_of(first, WIDE), span)
                state_ref[rows, :] = source_ref[rows, :]


def place_of(hop, rows, docs_ref):
    group = lax.axis_index("ctx")
    core = group & 1
    chip = group >> 1
    ends = [docs_ref[0]]
    for d in range(1, 7):
        ends.append(ends[-1] + docs_ref[d])
    return chip * 2 * rows, core, (chip - hop) * 2 * rows + core * rows, ends


def local_kernel(
    docs_ref, taps_ref, own_ref, other_ref, edge_ref, a_ref, b_ref,
    qp_ref, state_ref, done_ref,
    qx_ref, copied, start_ref, kx_ref, vx_ref, kp_ref,
):
    keys = kp_ref.shape[0]
    chip_row, core, block, ends = place_of(0, keys, docs_ref)
    taken = pltpu.make_async_copy(a_ref, kx_ref.at[pl.ds(HALO, keys), :], copied)
    taken.start()
    taps, _, key_taps = taps_ref.shape
    rim = (key_taps - 1) // 2
    done_ref[...] = jnp.zeros(done_ref.shape, jnp.float32)

    @pl.when(core == 0)
    def _():
        qx_ref[0:HALO, :] = edge_ref[HALO:, :].astype(jnp.float32)
        qx_ref[HALO : HALO + keys, :] = own_ref[0:keys, :].astype(jnp.float32)
        qx_ref[HALO + keys :, :] = other_ref[0:keys, :].astype(jnp.float32)

    @pl.when(core != 0)
    def _():
        qx_ref[0:HALO, :] = other_ref[keys:, :].astype(jnp.float32)
        qx_ref[HALO : HALO + keys, :] = other_ref[0:keys, :].astype(jnp.float32)
        qx_ref[HALO + keys :, :] = own_ref[0:keys, :].astype(jnp.float32)

    count = state_ref.shape[0]
    for u in range(taps):
        qp_ref[0:count, u * HEAD_DIM : (u + 1) * HEAD_DIM] = qx_ref[
            HALO - u : HALO - u + count, :
        ].astype(jnp.bfloat16)
    lane = lax.broadcasted_iota(jnp.int32, (8, 256), 1)
    for u in range(taps):
        base = jnp.zeros(lane.shape, jnp.float32)
        for t in range(key_taps):
            tap = taps_ref[u, 0, t] * SCALE
            if u == 0 and t == rim:
                tap = tap + SCALE
            base = jnp.where(lane == HALO + rim - t, tap, base)
        band = jnp.concatenate([base] * (GROUP // 8), axis=0)
        band = pltpu.roll(band, 0, 1, stride=1, stride_axis=0)
        high = band.astype(jnp.bfloat16)
        qp_ref[taps_at(qp_ref, 0, u)] = high
        qp_ref[taps_at(qp_ref, 1, u)] = (band - high.astype(jnp.float32)).astype(jnp.bfloat16)
    lane = lax.broadcasted_iota(jnp.int32, (count, 128), 1)
    state_ref[:, 0 : 2 * HEAD_DIM] = jnp.zeros((count, 2 * HEAD_DIM), jnp.float32)
    state_ref[:, 2 * HEAD_DIM :] = jnp.where(lane < 64, FLOOR, 0.0)
    lay_keys(None, b_ref, kx_ref, vx_ref)
    taken.wait()
    rest = (chip_row, block, ends, taps_ref, qp_ref, kx_ref, vx_ref, start_ref, state_ref)

    tiles = [n * BAND for n in range(keys // BAND)]
    past = block + keys - chip_row < count
    near(tiles[:TILES], *rest)

    @pl.when(past)
    def _():
        near(tiles[TILES:] + [keys], *rest)

    @pl.when(jnp.logical_not(past))
    def _():
        near(tiles[TILES:], *rest)

    convolve(True, block, 0, ends, qp_ref, kx_ref, kp_ref)
    far(4, chip_row, block, ends, qp_ref, kp_ref, vx_ref, state_ref, state_ref)


def hop_kernel(hop, last, docs_ref, taps_ref, qp_ref, a_ref, b_ref, state_in, *rest):
    if last:
        keep_ref, send_ref, start_ref, kx_ref, vx_ref, kp_ref, state_ref = rest
    else:
        state_ref, done_ref, start_ref, kx_ref, vx_ref, kp_ref = rest
        done_ref[...] = jnp.zeros(done_ref.shape, jnp.float32)
    keys = kp_ref.shape[0]
    chip_row, core, block, ends = place_of(hop, keys, docs_ref)
    first = hop == 1
    first_start = starts_of(chip_row, ends)
    active = block + keys > first_start
    if first:
        state_ref[...] = state_in[...]
    else:

        @pl.when(jnp.logical_not(active))
        def _():
            state_ref[...] = state_in[...]

    @pl.when(active)
    def _():
        lay_keys(a_ref, b_ref, kx_ref, vx_ref)
        if first:

            @pl.when(block + keys == chip_row)
            def _():
                near(
                    [keys], chip_row, block, ends, taps_ref, qp_ref, kx_ref, vx_ref, start_ref,
                    state_ref,
                )

        convolve(False, block, first_start, ends, qp_ref, kx_ref, kp_ref)
        source = state_ref if first else state_in
        far(2 if last else 4, chip_row, block, ends, qp_ref, kp_ref, vx_ref, source, state_ref)

    if last:
        for ref, side in ((keep_ref, core), (send_ref, 1 - core)):
            ref[...] = state_ref[pl.ds(pl.multiple_of(side * keys, keys), keys), :]


def join_kernel(keep_ref, other_ref, own_ref, cross_ref):
    wide = 2 * HEAD_DIM
    stats, more = keep_ref[:, wide:], other_ref[:, wide:]
    m_a, l_a = stats[:, 0:1], stats[:, 64:65]
    m_b, l_b = more[:, 0:1], more[:, 64:65]
    m = jnp.maximum(m_a, m_b)
    f_a, f_b = jnp.exp(m_a - m), jnp.exp(m_b - m)
    share = 1.0 / (l_a * f_a + l_b * f_b)
    f_a, f_b = f_a * share, f_b * share
    own_ref[...] = keep_ref[:, :HEAD_DIM] * f_a + other_ref[:, :HEAD_DIM] * f_b
    cross_ref[...] = (
        keep_ref[:, HEAD_DIM:wide] * f_a + other_ref[:, HEAD_DIM:wide] * f_b
    ).astype(jnp.bfloat16)


def finish_kernel(mixing_ref, own_ref, cross_ref, gain_ref, out_ref):
    mixed = mixing_ref[0] * own_ref[...] + mixing_ref[1] * cross_ref[...].astype(jnp.float32)
    mean = jnp.mean(mixed * mixed, axis=1, keepdims=True)
    out_ref[...] = (mixed * lax.rsqrt(mean + 1e-05) * gain_ref[...]).astype(jnp.bfloat16)


VMEM = pl.BlockSpec(memory_space=pltpu.VMEM)
SMEM = pl.BlockSpec(memory_space=pltpu.SMEM)


def call(kernel, specs, out, scratch, args, flops=0):
    shapes = [jax.ShapeDtypeStruct(shape, dtype) for shape, dtype in out]
    return pl.pallas_call(
        kernel,
        out_shape=shapes,
        in_specs=specs,
        out_specs=[VMEM] * len(shapes),
        scratch_shapes=scratch,
        cost_estimate=pl.CostEstimate(flops=8 * flops, bytes_accessed=4 << 20, transcendentals=0),
        compiler_params=pltpu.CompilerParams(vmem_limit_bytes=20 << 20),
    )(*args)


def body(queries, key_vectors, values, kernel, mixing, norm_gain, doc_lengths):
    rows = queries.shape[0]
    bf16, f32 = jnp.bfloat16, jnp.float32
    count = lax.axis_size("ctx")
    heads = lax.axis_size("head")
    taps = kernel.shape[1]
    width = taps * HEAD_DIM

    def permute(value, pairs):
        return lax.ppermute(value, "ctx", pairs)

    def onward(value):
        return permute(value, [(i, (i + 2) % count) for i in range(count)])

    def partner(value):
        return lax.ppermute(value, "head", [(i, i ^ (heads // 2)) for i in range(heads)])

    def step(value, by):
        return permute(value, [(i, (i + by) % count) for i in range(count)])

    other_values = partner(values)
    beyond = step(key_vectors[:HALO], -1)
    behind = step(jnp.concatenate([key_vectors[rows - HALO :], queries[rows - HALO :]]), 1)
    mine = jnp.concatenate([queries, behind[HALO:]])
    sibling = permute(mine, [(i, i ^ 1) for i in range(count)])
    by_tap = jnp.transpose(kernel, (1, 0, 2))
    ring_a = key_vectors
    ring_b = jnp.concatenate([values, other_values, behind[:HALO], beyond])
    state = [((2 * rows, 3 * HEAD_DIM), f32)]
    mark = [((8, 128), f32)]
    scratch = [
        pltpu.VMEM((TILES + 1, BAND // 2 + 8, GROUP), jnp.int32),
        pltpu.VMEM((rows + 128, HEAD_DIM), bf16),
        pltpu.VMEM((rows + 128, 2 * HEAD_DIM), bf16),
        pltpu.VMEM((rows, 2 * width), bf16),
    ]
    flops = 2 * 2 * rows * rows * (2 * width + 2 * HEAD_DIM)
    operand, running, done = call(
        local_kernel,
        [SMEM, SMEM, VMEM, VMEM, VMEM, pl.BlockSpec(memory_space=pltpu.HBM), VMEM],
        [((2 * rows + 2 * taps * GROUP * 256 // width, width), bf16)]
        + state
        + mark,
        [pltpu.VMEM((2 * rows + HALO, HEAD_DIM), f32), pltpu.SemaphoreType.DMA] + scratch,
        (doc_lengths, by_tap, mine, sibling, behind, ring_a, ring_b),
        flops=8 * flops,
    )
    for hop in range(1, HOPS + 1):
        ring_a, ring_b = onward(ring_a), onward(ring_b)
        if hop > 1:
            ring_a, _ = lax.optimization_barrier((ring_a, before))
        before = done
        ring_b, _ = lax.optimization_barrier((ring_b, done))
        last = hop == HOPS
        out = [((rows, 3 * HEAD_DIM), f32)] * 2 if last else state + mark
        extra = [pltpu.VMEM(shape, dtype) for shape, dtype in state] if last else []
        result = call(
            functools.partial(hop_kernel, hop, last),
            [SMEM, SMEM] + [VMEM] * 4,
            out,
            scratch + extra,
            (doc_lengths, by_tap, operand, ring_a, ring_b, running),
            flops=8 * flops,
        )
        if not last:
            running, done = result
    keep, send = result
    other = permute(send, [(i, i ^ 1) for i in range(count)])
    own, cross = call(
        join_kernel,
        [VMEM, VMEM],
        [((rows, HEAD_DIM), f32), ((rows, HEAD_DIM), bf16)],
        [],
        (keep, other),
    )
    (finished,) = call(
        finish_kernel,
        [SMEM, VMEM, VMEM, VMEM],
        [((rows, HEAD_DIM), bf16)],
        [],
        (mixing.reshape(-1), own, partner(cross), norm_gain.reshape(1, HEAD_DIM)),
    )
    return finished


def solution(mesh):
    return jax.shard_map(
        body,
        mesh=mesh,
        in_specs=(
            P("ctx", "head"),
            P("ctx", "head"),
            P("ctx", "head"),
            P("head", None, None),
            P("head", None),
            P("head"),
            P(),
        ),
        out_specs=P("ctx", "head"),
        check_vma=False,
    )
```

```python
import functools

import jax
import jax.numpy as jnp
from jax import lax
from jax.experimental import pallas as pl
from jax.experimental.pallas import tpu as pltpu
from jax.sharding import PartitionSpec as P

HEAD_DIM = 128
SCALE = HEAD_DIM ** (-0.5)
MASKED = -1e30
FLOOR = -1e20
HALO = 16
BAND = 64
TILES = 4
GROUP = 128
WIDE = 256
REACH = 10
HOPS = 4


def dot(a, b):
    return lax.dot_general(a, b, (((1,), (0,)), ((), ())), preferred_element_type=jnp.float32)


def dot_t(a, b):
    return lax.dot_general(a, b, (((1,), (1,)), ((), ())), preferred_element_type=jnp.float32)


def starts_of(position, ends):
    start = jnp.zeros_like(position)
    for end in ends:
        start = jnp.where(position >= end, end, start)
    return start


def widen(column, times):
    return jnp.concatenate([column] * times, axis=1) if times > 1 else column


def absorb(tiles, source_ref, state_ref):
    wide = 2 * HEAD_DIM
    done = []
    for rows, logits, values in tiles:
        m_old = source_ref[rows, wide : wide + 1]
        m_new = jnp.maximum(m_old, jnp.max(logits, axis=1, keepdims=True))
        weights = jnp.exp(logits - m_new)
        factor = jnp.exp(m_old - m_new)
        total = source_ref[rows, wide + 64 : wide + 65] * factor
        total = total + jnp.sum(weights, axis=1, keepdims=True)
        product = dot(weights.astype(jnp.bfloat16), values)
        product = source_ref[rows, 0:wide] * factor + product
        lane = lax.broadcasted_iota(jnp.int32, (logits.shape[0], 128), 1)
        done.append((rows, jnp.where(lane < 64, m_new, total), product))
    for rows, stats, product in done:
        state_ref[rows, 0:wide] = product
        state_ref[rows, wide:] = stats


def taps_at(qp_ref, rest, u):
    most = qp_ref.shape[1] // 256
    sets = qp_ref.shape[1] // HEAD_DIM // most
    row = qp_ref.shape[0] - (2 - rest) * sets * GROUP + u // most * GROUP
    return slice(row, row + GROUP), slice(u % most * 256, u % most * 256 + 256)


def lay_keys(a_ref, b_ref, kx_ref, vx_ref):
    keys = kx_ref.shape[0] - 128
    kx_ref[0:HALO, :] = b_ref[2 * keys : 2 * keys + HALO, :]
    if a_ref is not None:
        kx_ref[HALO : HALO + keys, :] = a_ref[...]
    kx_ref[HALO + keys : 2 * HALO + keys, :] = b_ref[2 * keys + HALO :, :]
    kx_ref[2 * HALO + keys :, :] = jnp.zeros_like(kx_ref[2 * HALO + keys :, :])
    vx_ref[0:HALO, :] = jnp.zeros((HALO, 2 * HEAD_DIM), jnp.bfloat16)
    vx_ref[HALO : HALO + keys, 0:HEAD_DIM] = b_ref[0:keys, :]
    vx_ref[HALO : HALO + keys, HEAD_DIM:] = b_ref[keys : 2 * keys, :]
    vx_ref[HALO + keys :, :] = jnp.zeros_like(vx_ref[HALO + keys :, :])


def near(tiles, chip_row, block, ends, taps_ref, qp_ref, kx_ref, vx_ref, start_ref, state_ref):
    keys = kx_ref.shape[0] - 128
    query_taps, _, key_taps = taps_ref.shape
    rim = (key_taps - 1) // 2
    half = BAND // 2
    shape = (half, GROUP)
    for n, a in enumerate(tiles):
        top = block + a
        one_start = starts_of(top + BAND - 1, ends)
        one = starts_of(top - 8, ends) == one_start

        @pl.when(one)
        def _(n=n, one_start=one_start):
            start_ref[n] = jnp.full(start_ref.shape[1:], one_start, jnp.int32)

        @pl.when(jnp.logical_not(one))
        def _(n=n, top=top):
            side = lax.broadcasted_iota(jnp.int32, start_ref.shape[1:], 1) >= 64
            position = top - 8 + lax.broadcasted_iota(jnp.int32, start_ref.shape[1:], 0)
            start_ref[n] = starts_of(position + jnp.where(side, half, 0), ends)

    lane = lax.broadcasted_iota(jnp.int32, shape, 1)
    left = lane < 64
    shift = jnp.where(left, 0, half)
    step = lax.broadcasted_iota(jnp.int32, shape, 0) + shift
    place = lane - HALO - shift
    behind = step - place
    work = []
    for n, a in enumerate(tiles):
        rows = pl.ds(pl.multiple_of(block - chip_row + a, 16), BAND)
        parts = [
            (pl.ds(pl.multiple_of(a + m, 16), 64), pl.ds(pl.multiple_of(block - chip_row + a + m, 16), half))
            for m in (0, half)
        ]
        stacked = jnp.concatenate(
            [
                qp_ref[part, u * HEAD_DIM : (u + 1) * HEAD_DIM]
                for _, part in parts
                for u in range(query_taps)
            ],
            axis=0,
        )
        window = jnp.concatenate([kx_ref[span, :] for span, _ in parts], axis=0)
        values = jnp.concatenate([vx_ref[span, :] for span, _ in parts], axis=0)
        work.append((n, rows, block + a + place, dot_t(stacked, window), values))
    done = []
    for n, rows, col, products, values in work:
        scores = []
        for u in range(query_taps):
            both = [products[(m * query_taps + u) * half :][:half] for m in (0, 1)]
            allowed = (behind >= u) & (col >= start_ref[n, 8 - u : 8 - u + half, :])
            scores.append(jnp.where(allowed, jnp.where(left, *both), 0.0))
        conv = None
        for t in range(key_taps):
            terms = None
            for u in range(query_taps):
                tap = taps_ref[u, 0, t] * SCALE
                if u == 0 and t == rim:
                    tap = tap + SCALE
                terms = scores[u] * tap if terms is None else terms + scores[u] * tap
            if t != rim:
                terms = pltpu.roll(terms, (t - rim) % GROUP, 1)
            conv = terms if conv is None else conv + terms
        inside = (col >= block) & (col < block + keys) & (col >= start_ref[n, 8 : 8 + half, :])
        inside = inside & (behind >= 0) & (behind < REACH)
        logits = jnp.concatenate(
            [
                jnp.where(inside & left, conv, MASKED),
                jnp.where(inside & jnp.logical_not(left), conv, MASKED),
            ],
            axis=0,
        )
        done.append((rows, logits, values))
    absorb(done, state_ref, state_ref)


def convolve(local, block, first_start, ends, qp_ref, kx_ref, kp_ref):
    total = kx_ref.shape[0]
    keys = kp_ref.shape[0]
    width = kp_ref.shape[1] // 2
    taps = width // HEAD_DIM
    depth = 256
    def put(g, u, done):
        top = done.astype(jnp.bfloat16)
        rest = (done - top.astype(jnp.float32)).astype(jnp.bfloat16)
        for n in range(done.shape[1] // HEAD_DIM):
            here = slice((g + n) * GROUP, (g + n + 1) * GROUP)
            lanes = slice(n * HEAD_DIM, (n + 1) * HEAD_DIM)
            kp_ref[here, u * HEAD_DIM : (u + 1) * HEAD_DIM] = top[:, lanes]
            kp_ref[here, width + u * HEAD_DIM : width + (u + 1) * HEAD_DIM] = rest[:, lanes]

    def whole():
        for g in range(0, keys // GROUP, 2):
            window = jnp.concatenate(
                [kx_ref[n * GROUP : n * GROUP + depth, :] for n in (g, g + 1)], axis=1
            )
            for u in range(taps):
                high, rest = (qp_ref[taps_at(qp_ref, n, u)] for n in (0, 1))
                put(g, u, dot(high, window) + dot(rest, window))

    def cut():
        for g in range(keys // GROUP):
            shape = (GROUP, depth)
            out = block + g * GROUP + lax.broadcasted_iota(jnp.int32, shape, 0)
            inp = block + g * GROUP - HALO + lax.broadcasted_iota(jnp.int32, shape, 1)
            keep = inp >= starts_of(out, ends)
            window = kx_ref[g * GROUP : g * GROUP + depth, :]
            for u in range(taps):
                high, rest = (
                    jnp.where(keep, qp_ref[taps_at(qp_ref, n, u)].astype(jnp.float32), 0.0).astype(
                        jnp.bfloat16
                    )
                    for n in (0, 1)
                )
                put(g, u, dot(high, window) + dot(rest, window))

    if local:
        unbroken = starts_of(block + keys - 1, ends) <= block - HALO

        @pl.when(unbroken)
        def _():
            whole()

        @pl.when(jnp.logical_not(unbroken))
        def _():
            cut()

        return
    place = block - HALO + lax.broadcasted_iota(jnp.int32, (total, HEAD_DIM), 0)
    kx_ref[...] = jnp.where(place >= first_start, kx_ref[...].astype(jnp.float32), 0.0).astype(
        jnp.bfloat16
    )
    whole()


def far(tiles_at_once, chip_row, block, ends, qp_ref, kp_ref, vx_ref, source_ref, state_ref):
    keys = kp_ref.shape[0]
    width = qp_ref.shape[1]
    span = tiles_at_once * WIDE

    @pl.loop(0, state_ref.shape[0] // span)
    def _(tile):
        first = tile * span
        top = chip_row + first
        needed = (top + span - 1 >= block + REACH) & (block + keys > starts_of(top, ends))

        @pl.when(needed)
        def _():
            tiles = []
            shape = (WIDE, GROUP)
            col = lax.broadcasted_iota(jnp.int32, (WIDE, keys), 1)
            for half in range(0, span, WIDE):
                rows = pl.ds(pl.multiple_of(first + half, WIDE), WIDE)
                query = qp_ref[rows, :]
                conv = dot_t(query, kp_ref[:, 0:width]) + dot_t(query, kp_ref[:, width:])
                row = top + half + lax.broadcasted_iota(jnp.int32, shape, 0)
                start = widen(starts_of(row, ends) - block, keys // GROUP)
                row = widen(row - (REACH + block), keys // GROUP)
                logits = jnp.where((col <= row) & (col >= start), conv, MASKED)
                tiles.append((rows, logits, vx_ref[HALO : HALO + keys, :]))
            absorb(tiles, source_ref, state_ref)

        if source_ref is not state_ref:

            @pl.when(jnp.logical_not(needed))
            def _():
                rows = pl.ds(pl.multiple_of(first, WIDE), span)
                state_ref[rows, :] = source_ref[rows, :]


def place_of(hop, rows, docs_ref):
    group = lax.axis_index("ctx")
    core = group & 1
    chip = group >> 1
    ends = [docs_ref[0]]
    for d in range(1, 7):
        ends.append(ends[-1] + docs_ref[d])
    return chip * 2 * rows, core, (chip - hop) * 2 * rows + core * rows, ends


def local_kernel(
    docs_ref, taps_ref, own_ref, other_ref, edge_ref, a_ref, b_ref,
    qp_ref, state_ref, done_ref,
    qx_ref, copied, start_ref, kx_ref, vx_ref, kp_ref,
):
    keys = kp_ref.shape[0]
    chip_row, core, block, ends = place_of(0, keys, docs_ref)
    taken = pltpu.make_async_copy(a_ref, kx_ref.at[pl.ds(HALO, keys), :], copied)
    taken.start()
    taps, _, key_taps = taps_ref.shape
    rim = (key_taps - 1) // 2
    done_ref[...] = jnp.zeros(done_ref.shape, jnp.float32)

    @pl.when(core == 0)
    def _():
        qx_ref[0:HALO, :] = edge_ref[HALO:, :].astype(jnp.float32)
        qx_ref[HALO : HALO + keys, :] = own_ref[0:keys, :].astype(jnp.float32)
        qx_ref[HALO + keys :, :] = other_ref[0:keys, :].astype(jnp.float32)

    @pl.when(core != 0)
    def _():
        qx_ref[0:HALO, :] = other_ref[keys:, :].astype(jnp.float32)
        qx_ref[HALO : HALO + keys, :] = other_ref[0:keys, :].astype(jnp.float32)
        qx_ref[HALO + keys :, :] = own_ref[0:keys, :].astype(jnp.float32)

    count = state_ref.shape[0]
    for u in range(taps):
        qp_ref[0:count, u * HEAD_DIM : (u + 1) * HEAD_DIM] = qx_ref[
            HALO - u : HALO - u + count, :
        ].astype(jnp.bfloat16)
    lane = lax.broadcasted_iota(jnp.int32, (8, 256), 1)
    for u in range(taps):
        base = jnp.zeros(lane.shape, jnp.float32)
        for t in range(key_taps):
            tap = taps_ref[u, 0, t] * SCALE
            if u == 0 and t == rim:
                tap = tap + SCALE
            base = jnp.where(lane == HALO + rim - t, tap, base)
        band = jnp.concatenate([base] * (GROUP // 8), axis=0)
        band = pltpu.roll(band, 0, 1, stride=1, stride_axis=0)
        high = band.astype(jnp.bfloat16)
        qp_ref[taps_at(qp_ref, 0, u)] = high
        qp_ref[taps_at(qp_ref, 1, u)] = (band - high.astype(jnp.float32)).astype(jnp.bfloat16)
    lane = lax.broadcasted_iota(jnp.int32, (count, 128), 1)
    state_ref[:, 0 : 2 * HEAD_DIM] = jnp.zeros((count, 2 * HEAD_DIM), jnp.float32)
    state_ref[:, 2 * HEAD_DIM :] = jnp.where(lane < 64, FLOOR, 0.0)
    lay_keys(None, b_ref, kx_ref, vx_ref)
    taken.wait()
    rest = (chip_row, block, ends, taps_ref, qp_ref, kx_ref, vx_ref, start_ref, state_ref)

    tiles = [n * BAND for n in range(keys // BAND)]
    past = block + keys - chip_row < count
    near(tiles[:TILES], *rest)

    @pl.when(past)
    def _():
        near(tiles[TILES:] + [keys], *rest)

    @pl.when(jnp.logical_not(past))
    def _():
        near(tiles[TILES:], *rest)

    convolve(True, block, 0, ends, qp_ref, kx_ref, kp_ref)
    far(4, chip_row, block, ends, qp_ref, kp_ref, vx_ref, state_ref, state_ref)


def hop_kernel(hop, last, docs_ref, taps_ref, qp_ref, a_ref, b_ref, state_in, *rest):
    if last:
        keep_ref, send_ref, start_ref, kx_ref, vx_ref, kp_ref, state_ref = rest
    else:
        state_ref, done_ref, start_ref, kx_ref, vx_ref, kp_ref = rest
        done_ref[...] = jnp.zeros(done_ref.shape, jnp.float32)
    keys = kp_ref.shape[0]
    chip_row, core, block, ends = place_of(hop, keys, docs_ref)
    first = hop == 1
    first_start = starts_of(chip_row, ends)
    active = block + keys > first_start
    if first:
        state_ref[...] = state_in[...]
    else:

        @pl.when(jnp.logical_not(active))
        def _():
            state_ref[...] = state_in[...]

    @pl.when(active)
    def _():
        lay_keys(a_ref, b_ref, kx_ref, vx_ref)
        if first:

            @pl.when(block + keys == chip_row)
            def _():
                near(
                    [keys], chip_row, block, ends, taps_ref, qp_ref, kx_ref, vx_ref, start_ref,
                    state_ref,
                )

        convolve(False, block, first_start, ends, qp_ref, kx_ref, kp_ref)
        source = state_ref if first else state_in
        far(4, chip_row, block, ends, qp_ref, kp_ref, vx_ref, source, state_ref)

    if last:
        for ref, side in ((keep_ref, core), (send_ref, 1 - core)):
            ref[...] = state_ref[pl.ds(pl.multiple_of(side * keys, keys), keys), :]


def join_kernel(keep_ref, other_ref, own_ref, cross_ref):
    wide = 2 * HEAD_DIM
    stats, more = keep_ref[:, wide:], other_ref[:, wide:]
    m_a, l_a = stats[:, 0:1], stats[:, 64:65]
    m_b, l_b = more[:, 0:1], more[:, 64:65]
    m = jnp.maximum(m_a, m_b)
    f_a, f_b = jnp.exp(m_a - m), jnp.exp(m_b - m)
    share = 1.0 / (l_a * f_a + l_b * f_b)
    f_a, f_b = f_a * share, f_b * share
    own_ref[...] = keep_ref[:, :HEAD_DIM] * f_a + other_ref[:, :HEAD_DIM] * f_b
    cross_ref[...] = (
        keep_ref[:, HEAD_DIM:wide] * f_a + other_ref[:, HEAD_DIM:wide] * f_b
    ).astype(jnp.bfloat16)


def finish_kernel(mixing_ref, own_ref, cross_ref, gain_ref, out_ref):
    mixed = mixing_ref[0] * own_ref[...] + mixing_ref[1] * cross_ref[...].astype(jnp.float32)
    mean = jnp.mean(mixed * mixed, axis=1, keepdims=True)
    out_ref[...] = (mixed * lax.rsqrt(mean + 1e-05) * gain_ref[...]).astype(jnp.bfloat16)


VMEM = pl.BlockSpec(memory_space=pltpu.VMEM)
SMEM = pl.BlockSpec(memory_space=pltpu.SMEM)


def call(kernel, specs, out, scratch, args, flops=0):
    shapes = [jax.ShapeDtypeStruct(shape, dtype) for shape, dtype in out]
    return pl.pallas_call(
        kernel,
        out_shape=shapes,
        in_specs=specs,
        out_specs=[VMEM] * len(shapes),
        scratch_shapes=scratch,
        cost_estimate=pl.CostEstimate(flops=8 * flops, bytes_accessed=4 << 20, transcendentals=0),
        compiler_params=pltpu.CompilerParams(vmem_limit_bytes=20 << 20),
    )(*args)


def body(queries, key_vectors, values, kernel, mixing, norm_gain, doc_lengths):
    rows = queries.shape[0]
    bf16, f32 = jnp.bfloat16, jnp.float32
    count = lax.axis_size("ctx")
    heads = lax.axis_size("head")
    taps = kernel.shape[1]
    width = taps * HEAD_DIM

    def permute(value, pairs):
        return lax.ppermute(value, "ctx", pairs)

    def onward(value):
        return permute(value, [(i, (i + 2) % count) for i in range(count)])

    def partner(value):
        return lax.ppermute(value, "head", [(i, i ^ (heads // 2)) for i in range(heads)])

    def step(value, by):
        return permute(value, [(i, (i + by) % count) for i in range(count)])

    other_values = partner(values)
    beyond = step(key_vectors[:HALO], -1)
    behind = step(jnp.concatenate([key_vectors[rows - HALO :], queries[rows - HALO :]]), 1)
    mine = jnp.concatenate([queries, behind[HALO:]])
    sibling = permute(mine, [(i, i ^ 1) for i in range(count)])
    by_tap = jnp.transpose(kernel, (1, 0, 2))
    ring_a = key_vectors
    ring_b = jnp.concatenate([values, other_values, behind[:HALO], beyond])
    state = [((2 * rows, 3 * HEAD_DIM), f32)]
    mark = [((8, 128), f32)]
    scratch = [
        pltpu.VMEM((TILES + 1, BAND // 2 + 8, GROUP), jnp.int32),
        pltpu.VMEM((rows + 128, HEAD_DIM), bf16),
        pltpu.VMEM((rows + 128, 2 * HEAD_DIM), bf16),
        pltpu.VMEM((rows, 2 * width), bf16),
    ]
    flops = 2 * 2 * rows * rows * (2 * width + 2 * HEAD_DIM)
    operand, running, done = call(
        local_kernel,
        [SMEM, SMEM, VMEM, VMEM, VMEM, pl.BlockSpec(memory_space=pltpu.HBM), VMEM],
        [((2 * rows + 2 * taps * GROUP * 256 // width, width), bf16)]
        + state
        + mark,
        [pltpu.VMEM((2 * rows + HALO, HEAD_DIM), f32), pltpu.SemaphoreType.DMA] + scratch,
        (doc_lengths, by_tap, mine, sibling, behind, ring_a, ring_b),
        flops=8 * flops,
    )
    for hop in range(1, HOPS + 1):
        ring_a, ring_b = onward(ring_a), onward(ring_b)
        ring_a, _ = lax.optimization_barrier((ring_a, done))
        ring_b, _ = lax.optimization_barrier((ring_b, done))
        last = hop == HOPS
        out = [((rows, 3 * HEAD_DIM), f32)] * 2 if last else state + mark
        extra = [pltpu.VMEM(shape, dtype) for shape, dtype in state] if last else []
        result = call(
            functools.partial(hop_kernel, hop, last),
            [SMEM, SMEM] + [VMEM] * 4,
            out,
            scratch + extra,
            (doc_lengths, by_tap, operand, ring_a, ring_b, running),
            flops=8 * flops,
        )
        if not last:
            running, done = result
    keep, send = result
    other = permute(send, [(i, i ^ 1) for i in range(count)])
    own, cross = call(
        join_kernel,
        [VMEM, VMEM],
        [((rows, HEAD_DIM), f32), ((rows, HEAD_DIM), bf16)],
        [],
        (keep, other),
    )
    (finished,) = call(
        finish_kernel,
        [SMEM, VMEM, VMEM, VMEM],
        [((rows, HEAD_DIM), bf16)],
        [],
        (mixing.reshape(-1), own, partner(cross), norm_gain.reshape(1, HEAD_DIM)),
    )
    return finished


def solution(mesh):
    return jax.shard_map(
        body,
        mesh=mesh,
        in_specs=(
            P("ctx", "head"),
            P("ctx", "head"),
            P("ctx", "head"),
            P("head", None, None),
            P("head", None),
            P("head"),
            P(),
        ),
        out_specs=P("ctx", "head"),
        check_vma=False,
    )
```
